512 devices in a mesh: img: 8 (over z_hi, x), patch: 64 (over z_lo, y, core).
Axes of the slice: x: 4, y: 8, z: 8 (z_hi: 2, z_lo: 4; z = z_hi * 4 + z_lo), core: 2. Of those that a mesh axis runs over, the one named last changes fastest.
Arguments:
- hidden_in: bfloat16 [16, 3072, 1280], P('img', 'patch'), parts along dimension 0, may hold values from -25 to 25
- gn_gain: float32 [1280], replicated, may hold values from 0.1 to 1.9
- gn_bias: float32 [1280], replicated, may hold values from -3 to 3
- stale_local: float32 [16, 64, 2, 32], P('img', 'patch'), parts along dimension 0, may hold values from -9600 to 480000, as said below
- w_qkv: bfloat16 [1280, 1920], P('patch'), may hold values from -0.15625 to 0.15625
- stale_values: bfloat16 [16, 3072, 1280], P('img', 'patch'), parts along dimension 0, may hold values from -1 to 1
- stale_scales: bfloat16 [16, 3072, 2], P('img', 'patch'), parts along dimension 0, may hold values from 1 to 200
Outputs:
- attended: bfloat16 [16, 3072, 640], P('img', 'patch'), parts along dimension 0
- fresh_values: bfloat16 [16, 3072, 1280], P('img', 'patch'), parts along dimension 0
- fresh_scales: bfloat16 [16, 3072, 2], P('img', 'patch'), parts along dimension 0
- gn_totals: float32 [16, 2, 32], P('img'), parts along dimension 0
The draws below stay inside these ranges and needn't reach their ends.
There are 8 independent parts, one for each index of `img`. The reference program is written for one: setup_inputs(seed, part) draws one part's arguments, and reference() takes and returns one part's arrays. A program takes and returns all parts, laid end to end along the dimension named above; an argument that names none is the same for every part. Nothing has to cross between parts.
Inputs may be any that keep to these rules, and one draw needn't show every extreme that they name: stale_local[b, p, 1] is positive.
All inputs are finite; a program needn't handle non-finite values. Where the reference program divides by a largest or mean magnitude, that divisor is 1e-20 or more.
Results may differ from the reference program's by a relative error of at most 0.0075.
The reference program's roundings to bfloat16 on the way (of `normed`, `projected` and `weights`) count: a program that leaves them out, or rounds other values in their place, can miss the bound.
Values may be sent and summed in bfloat16 or wider, within the bound.
A program may use at most 128 MiB of HBM per device.

```python
import jax
import jax.numpy as jnp
from jax import lax

D = 1280
HEADS = 10
HEAD_DIM = 64
GROUPS = 32
H = 64
W = 48
IMGS = 2
CPG = 40
TOK_DEV = 48
TOKENS = 3072
N_PATCH = 64


def draw_hidden_in(key, part):
    key = jax.random.fold_in(key, 11)
    key_noise, key_shift = jax.random.split(key)
    row_frac = (jnp.arange(TOKENS) // W).astype(jnp.float32) / (H - 1)
    noise_base = jnp.clip(jax.random.normal(key_noise, (IMGS, TOKENS, D), jnp.float32), -6.0, 6.0)
    chan_shift = jax.random.uniform(key_shift, (IMGS, 1, D), jnp.float32, -0.5, 0.5)
    row_rise = jnp.exp(row_frac * jnp.log(3.0))
    return ((noise_base + chan_shift) * row_rise[None, :, None]).astype(jnp.bfloat16)


def draw_stale_local(key, part):
    key = jax.random.fold_in(key, 12)
    key_sums, key_squares = jax.random.split(key)
    patch_frac = jnp.arange(N_PATCH).astype(jnp.float32) / (N_PATCH - 1)
    cells = float(TOK_DEV * CPG)
    patch_rise = jnp.exp(patch_frac * jnp.log(3.0))
    squares = jax.random.uniform(key_squares, (IMGS, N_PATCH, GROUPS), jnp.float32, 0.8, 1.6)
    sums = jax.random.uniform(key_sums, (IMGS, N_PATCH, GROUPS), jnp.float32, -0.5, 0.5)
    sums = cells * patch_rise[None, :, None] * sums
    squares = cells * (patch_rise * patch_rise)[None, :, None] * squares
    return jnp.stack([sums, squares], axis=2)


def draw_stale_scales(key, part):
    key = jax.random.fold_in(key, 13)
    key_base = jax.random.fold_in(key, 0)
    base = jnp.exp(jax.random.uniform(key_base, (IMGS, TOKENS, 2), jnp.float32, 0.0, jnp.log(8.0)))
    return base.astype(jnp.bfloat16)


def level_of(rng, shape, cuts, least, high):
    def one(axis_at, blocks):
        steps = jax.random.uniform(jax.random.fold_in(jax.random.fold_in(rng, 6), axis_at), (blocks,), jnp.float32, least / len(cuts), high / len(cuts))
        return jnp.repeat(jnp.exp(steps), shape[axis_at] // blocks).reshape((-1,) + (1,) * (len(shape) - axis_at - 1))

    loudness = one(*cuts[0])
    for cut in cuts[1:]:
        loudness = loudness * one(*cut)
    return loudness


def gaussian(rng, dims, deviation, limit, pieces=(), kind=jnp.bfloat16):
    drawn = deviation * jax.random.normal(rng, dims, jnp.float32)
    if pieces:
        drawn = drawn * level_of(rng, dims, pieces, -0.22, 0.18)
    return jnp.clip(drawn, -limit, limit).astype(kind)


def setup_inputs(seed: int = 0, part: int = 0) -> dict:
    seeds = jax.random.split(jax.random.key(seed), 8)
    part_keys = jax.random.split(jax.random.fold_in(seeds[7], part), 8)
    hidden_in = draw_hidden_in(jax.random.fold_in(jax.random.fold_in(seeds[7], part), 71), part)
    gn_gain = jnp.clip(1.0 + 0.18 * jax.random.normal(seeds[1], (D,), jnp.float32), 0.1, 1.9)
    gn_bias = gaussian(seeds[2], (D,), 0.5, 3.0, (), jnp.float32)
    stale_local = draw_stale_local(jax.random.fold_in(jax.random.fold_in(seeds[7], part), 71), part)
    w_qkv = gaussian(seeds[4], (D, 3 * HEADS * HEAD_DIM), D ** -0.5, 0.15625, ((0, 64),))
    stale_values = jnp.clip(jax.random.uniform(part_keys[5], (IMGS, TOKENS, 2 * HEADS * HEAD_DIM), jnp.float32, -1.0, 1.0) * level_of(part_keys[5], (IMGS, TOKENS, 2 * HEADS * HEAD_DIM), ((1, 64),), -0.4, 0.0), -1.0, 1.0).astype(jnp.bfloat16)
    stale_scales = draw_stale_scales(jax.random.fold_in(jax.random.fold_in(seeds[7], part), 71), part)
    return {"hidden_in": hidden_in, "gn_gain": gn_gain, "gn_bias": gn_bias, "stale_local": stale_local, "w_qkv": w_qkv, "stale_values": stale_values, "stale_scales": stale_scales}


def quantize(block):
    magnitude = lax.optimization_barrier(jnp.max(jnp.abs(block.astype(jnp.float32)), axis=-1)) + 1e-06
    codes = (block.astype(jnp.float32) / magnitude[..., None]).astype(jnp.bfloat16)
    return (codes, magnitude)

def reference(hidden_in, gn_gain, gn_bias, stale_local, w_qkv, stale_values, stale_scales):
    head_cols = HEADS * HEAD_DIM
    features = hidden_in.astype(jnp.float32).reshape(IMGS, N_PATCH, TOK_DEV, GROUPS, CPG)
    fresh_sums = jnp.stack([lax.optimization_barrier(jnp.sum(features, axis=(2, 4))), lax.optimization_barrier(jnp.sum(features * features, axis=(2, 4)))], axis=2)
    used_sums = lax.optimization_barrier(jnp.sum(stale_local, axis=1))[:, None] - stale_local + fresh_sums
    cell_count = float(TOKENS * CPG)
    group_mean = used_sums[:, :, 0] / cell_count
    group_var = used_sums[:, :, 1] / cell_count - group_mean * group_mean
    normed = (features - group_mean[:, :, None, :, None]) * lax.rsqrt(group_var + 1e-05)[:, :, None, :, None]
    normed = (normed.reshape(IMGS, TOKENS, D) * gn_gain + gn_bias).astype(jnp.bfloat16)
    projected = jnp.dot(normed.reshape(IMGS * TOKENS, D), w_qkv, preferred_element_type=jnp.float32).astype(jnp.bfloat16)
    projected = projected.reshape(IMGS, TOKENS, 3 * head_cols)
    queries = projected[:, :, :head_cols]
    fresh_keys = projected[:, :, head_cols:2 * head_cols]
    fresh_vals = projected[:, :, 2 * head_cols:]
    key_codes, key_scale = quantize(fresh_keys)
    value_codes, value_scale = quantize(fresh_vals)
    fresh_values = jnp.concatenate([key_codes, value_codes], axis=2)
    fresh_scales = jnp.stack([key_scale, value_scale], axis=2).astype(jnp.bfloat16)
    gn_totals = lax.optimization_barrier(jnp.sum(fresh_sums, axis=1))
    stale_keys = stale_values[:, :, :head_cols]
    stale_vals = stale_values[:, :, head_cols:]
    scale_keys = stale_scales[:, :, 0].astype(jnp.float32)
    scale_vals = stale_scales[:, :, 1].astype(jnp.float32)
    ones_row = jnp.ones((IMGS, TOK_DEV), jnp.float32)

    def attend_patch(patch_id):
        row_first = (patch_id * TOK_DEV).astype(jnp.int32)
        anchor = jnp.zeros((), jnp.int32)
        own_queries = lax.dynamic_slice(queries, (anchor, row_first, anchor), (IMGS, TOK_DEV, head_cols)).reshape(IMGS, TOK_DEV, HEADS, HEAD_DIM)
        own_keys = lax.dynamic_slice(fresh_keys, (anchor, row_first, anchor), (IMGS, TOK_DEV, head_cols))
        own_vals = lax.dynamic_slice(fresh_vals, (anchor, row_first, anchor), (IMGS, TOK_DEV, head_cols))
        all_keys = lax.dynamic_update_slice(stale_keys, own_keys, (anchor, row_first, anchor)).reshape(IMGS, TOKENS, HEADS, HEAD_DIM)
        all_vals = lax.dynamic_update_slice(stale_vals, own_vals, (anchor, row_first, anchor)).reshape(IMGS, TOKENS, HEADS, HEAD_DIM)
        key_factor = lax.dynamic_update_slice(scale_keys, ones_row, (anchor, row_first))
        value_factor = lax.dynamic_update_slice(scale_vals, ones_row, (anchor, row_first))
        scores = jnp.einsum('bqhd,bkhd->bhqk', own_queries.astype(jnp.float32), all_keys.astype(jnp.float32)) * key_factor[:, None, None, :] * 0.125
        top_score = lax.optimization_barrier(jnp.max(scores, axis=3, keepdims=True))
        lifted = jnp.exp(scores - top_score)
        denominator = lax.optimization_barrier(jnp.sum(lifted, axis=3))
        weights = (lifted * value_factor[:, None, None, :]).astype(jnp.bfloat16)
        mixed = jnp.einsum('bhqk,bkhd->bhqd', weights.astype(jnp.float32), all_vals.astype(jnp.float32)) / denominator[..., None]
        return jnp.transpose(mixed, (0, 2, 1, 3)).reshape(IMGS, TOK_DEV, head_cols).astype(jnp.bfloat16)
    attended = lax.map(attend_patch, jnp.arange(N_PATCH, dtype=jnp.int32))
    attended = jnp.transpose(attended, (1, 0, 2, 3)).reshape(IMGS, TOKENS, head_cols)
    return (attended, fresh_values, fresh_scales, gn_totals)
```

```python
import jax
import jax.numpy as jnp
from jax import lax
from jax.experimental import pallas as pl
from jax.experimental.pallas import tpu as pltpu
from jax.sharding import PartitionSpec as P

HEADS = 10
HEAD_DIM = 64
GROUPS = 32
D = 1280
CPG = 40
ROWS = 48
NY = 8
NZ = 4
NX = 4
QROWS = NY * ROWS
UNITS = 3
CHUNK = UNITS * ROWS + 16
WCOLS = 640
CELLS = 122880.0
BIG_NEG = -1e30
OFF = (0, 1, -1, 2, -2, 3, -3, 4)
KV_GROUPS = ((0, 3), (3, 2), (5, 3))
MESH = pl.DeviceIdType.MESH
F32 = jnp.float32
BF16 = jnp.bfloat16


def head_of(group, unit):
    return min(UNITS * group + unit, HEADS - 1)


def lane_low(shape):
    return lax.broadcasted_iota(jnp.int32, shape, 1) < HEAD_DIM


def join_halves(low, low_high, high, high_high):
    left = pltpu.roll(low, HEAD_DIM, 1) if low_high else low
    right = high if high_high else pltpu.roll(high, HEAD_DIM, 1)
    return jnp.where(lane_low(left.shape), left, right)


def kernel(
    hid_ref,
    gain_ref,
    bias_ref,
    stale_ref,
    w_ref,
    codes_ref,
    scales_ref,
    att_ref,
    fvals_ref,
    fscales_ref,
    totals_ref,
    kvs,
    kv,
    kv2,
    kvf,
    xbuf,
    xn,
    st,
    stbuf,
    stsib,
    stz,
    w32,
    wpack,
    w0,
    w80,
    wbuf,
    qbuf,
    mask_diag,
    mask_off,
    m_ref,
    l_ref,
    acc_ref,
    fsend,
    fhome,
    asend,
    ahome,
    kvy_s,
    kvy_r,
    kvup_s,
    kvdn_s,
    kvz_r,
    kvsib_s,
    kvsib_r,
    x_s,
    x_r,
    sty_s,
    sty_r,
    stsib_s,
    stsib_r,
    stz_s,
    stz_r,
    p0_s,
    p0_r,
    wy_s,
    wy_r,
    wz_s,
    wz_r,
    wx_s,
    wx_r,
    ws_s,
    ws_r,
    f_s,
    f_r,
    a_s,
    a_r,
):
    img = lax.axis_index("img")
    patch = lax.axis_index("patch")
    x = img % NX
    img_base = img - x
    z = patch // (2 * NY)
    y = (patch // 2) % NY
    c = patch % 2

    def dev(y_at=None, z_at=None, c_at=None, x_at=None):
        yy = y if y_at is None else y_at
        zz = z if z_at is None else z_at
        cc = c if c_at is None else c_at
        xx = x if x_at is None else x_at
        return {"img": img_base + xx, "patch": (zz * NY + yy) * 2 + cc}

    sib = dev(c_at=1 - c)
    y_peers = [dev(y_at=(y + k) % NY) for k in range(1, NY)]
    z_peers = [dev(z_at=(z + k) % NZ) for k in range(1, NZ)]
    x_peers = [dev(x_at=(x + k) % NX) for k in range(1, NX)]
    y_twin = y + 1 - 2 * (y % 2)
    diag = dev(y_at=y_twin, c_at=1 - c)
    everyone = y_peers + z_peers + x_peers + [sib, diag]

    barrier = pltpu.get_barrier_semaphore()
    for peer in everyone:
        pl.semaphore_signal(barrier, inc=1, device_id=peer, device_id_type=MESH)

    img_b = y % 2
    active = (y // 2) == x
    four = (y % 2) * 2 + c
    w_core = c == (y // 2) % 2

    pending = []

    def send(src, dst, s_sem, r_sem, peer, when=None):
        copy = pltpu.make_async_remote_copy(
            src_ref=src, dst_ref=dst, send_sem=s_sem, recv_sem=r_sem, device_id=peer, device_id_type=MESH
        )

        def start():
            copy.start()

        def finish():
            copy.wait_send()

        if when is None:
            start()
            pending.append(finish)
        else:
            pl.when(when)(start)
            pending.append(lambda: pl.when(when)(finish))

    def received(dst, s_sem, r_sem):
        pltpu.make_async_remote_copy(
            src_ref=dst, dst_ref=dst, send_sem=s_sem, recv_sem=r_sem, device_id=sib, device_id_type=MESH
        ).wait_recv()

    @pl.when(active)
    def _():
        w32[...] = jnp.zeros_like(w32)
        w32[0:20, :] = w_ref[...].astype(F32)

        def piece(block, head):
            unit = block * HEADS + head
            return w32[:, (unit // 2) * 128 : (unit // 2) * 128 + 128], unit % 2 == 1

        for g in range(4):
            h = [head_of(g, s) for s in range(UNITS)]
            plan = [((1, h[s]), (2, h[s])) for s in range(UNITS)]
            plan += [((0, h[0]), (0, h[1])), ((0, h[2]), (0, h[2]))]
            for t, (first, second) in enumerate(plan):
                a, a_high = piece(*first)
                b, b_high = piece(*second)
                wpack[g, :, t * 128 : t * 128 + 128] = join_halves(a, a_high, b, b_high).astype(BF16)

    for b in range(2):
        lane16 = lax.broadcasted_iota(jnp.int32, (16, 128), 1)
        sc = scales_ref[b].astype(F32)
        tile = jnp.zeros((16, 128), F32)
        for t in range(3):
            for f in range(2):
                col = sc[t * 16 : t * 16 + 16, f : f + 1]
                tile = jnp.where(lane16 == 2 * t + f, col, tile)
        tile = tile.astype(BF16)
        packed = {}
        for h in range(HEADS):
            k_tile = codes_ref[b, :, (h // 2) * 128 : (h // 2) * 128 + 128].astype(F32)
            v_tile = codes_ref[b, :, 640 + (h // 2) * 128 : 640 + (h // 2) * 128 + 128].astype(F32)
            odd = h % 2 == 1
            packed[h] = join_halves(k_tile, odd, v_tile, odd).astype(BF16)
        for g in range(4):
            for s in range(UNITS):
                kvs[2 * g + b, s * ROWS : (s + 1) * ROWS, :] = packed[head_of(g, s)]
            kvs[2 * g + b, UNITS * ROWS : CHUNK, :] = tile

    sub = lax.broadcasted_iota(jnp.int32, (GROUPS, D), 0) * CPG
    lane = lax.broadcasted_iota(jnp.int32, (GROUPS, D), 1)
    spread = jnp.where((lane >= sub) & (lane < sub + CPG), 1.0, 0.0).astype(F32)
    col_sums = []
    for b in range(2):
        feats = hid_ref[b].astype(F32)
        col_sums.append(jnp.sum(feats, axis=0, keepdims=True))
        col_sums.append(jnp.sum(feats * feats, axis=0, keepdims=True))
    col_sums = jnp.concatenate(col_sums, axis=0)
    fresh = lax.dot_general(
        col_sums, spread, (((1,), (1,)), ((), ())), precision=lax.Precision.HIGHEST, preferred_element_type=F32
    )
    st[...] = jnp.zeros_like(st)
    st[0:4, 0:GROUPS] = stale_ref[...]
    st[4:8, 0:GROUPS] = fresh
    stbuf[y] = st[...]

    kv[z, c, 0] = kvs[y]
    xbuf[0] = hid_ref[img_b]

    pl.semaphore_wait(barrier, len(everyone))

    for j in range(4):
        peer = dev(y_at=y - y % 2 + j // 2, c_at=j % 2)
        send(wpack.at[j], w0.at[pl.ds(pl.multiple_of(four * 32, 32), 32)], p0_s.at[j], p0_r.at[four], peer, active & (four != j))
    for i in range(1, NY):
        send(kvs.at[(y - OFF[i]) % NY], kv.at[z, c, i], kvy_s.at[i], kvy_r.at[i], dev(y_at=(y - OFF[i]) % NY))
    for k in range(1, NY):
        send(st, stbuf.at[y], sty_s.at[k], sty_r.at[y], dev(y_at=(y + k) % NY))
    for i in range(1, NY):
        dest = (y - OFF[i]) % NY
        send(hid_ref.at[dest % 2], xbuf.at[i], x_s.at[i], x_r.at[i], dev(y_at=dest))

    for i in range(NY):
        lane_q = lax.broadcasted_iota(jnp.int32, (ROWS, QROWS), 1)
        same = (lane_q >= i * ROWS) & (lane_q < (i + 1) * ROWS)
        mask_diag[i * ROWS : (i + 1) * ROWS, :] = jnp.where(same, 0.0, BIG_NEG)
        mask_off[i * ROWS : (i + 1) * ROWS, :] = jnp.where(same, BIG_NEG, 0.0)

    w_rows = pl.ds(pl.multiple_of((z * 4 + x) * 80, 80), 80)
    for j in range(4):

        @pl.when(active & (four != j))
        def _(j=j):
            received(w0.at[pl.ds(j * 32, 32)], p0_s.at[j], p0_r.at[j])

    @pl.when(active)
    def _():
        w0[pl.ds(pl.multiple_of(four * 32, 32), 32), :] = wpack[four]
        row = lax.broadcasted_iota(jnp.int32, (80, 128), 0)
        col = lax.broadcasted_iota(jnp.int32, (80, 128), 1)
        hit = jnp.zeros((80, 128), F32)
        for a in range(4):
            hit = jnp.where((row >= 20 * a) & (row < 20 * a + 20) & (col == row + 12 * a), 1.0, hit)
        w80[...] = jnp.dot(hit.astype(BF16), w0[...], preferred_element_type=F32).astype(BF16)

    for k in range(2):
        plane = 2 * four + k

        @pl.when(active & (plane == y))
        def _():
            wbuf[w_rows, :] = w80[...]

        send(w80, wbuf.at[w_rows], wy_s.at[k], wy_r.at[0], dev(y_at=plane), active & (plane != y))

    def kv_part(zz, cc, grp):
        first, count = KV_GROUPS[grp]
        return kv.at[zz, cc, pl.ds(first, count)]

    def kv_forward(zz, grp, up, down):
        part = kv_part(zz, c, grp)
        if up is not None:
            send(part, part, kvup_s.at[zz, grp], kvz_r.at[zz, grp], dev(z_at=jnp.minimum(z + 1, NZ - 1)), up)
        if down is not None:
            send(part, part, kvdn_s.at[zz, grp], kvz_r.at[zz, grp], dev(z_at=jnp.maximum(z - 1, 0)), down)

    def kv_own(grp):
        first, count = KV_GROUPS[grp]
        for i in range(first, first + count):
            if i > 0:
                received(kv.at[z, c, i], kvy_s.at[i], kvy_r.at[i])
        kv_forward(z, grp, z < NZ - 1, z > 0)
        part = kv_part(z, c, grp)
        send(part, part, kvsib_s.at[z, grp], kvsib_r.at[z, grp], sib)

    def kv_relay(dist, grp):
        for sign in (-1, 1):
            src_z = z + sign * dist
            there = (src_z >= 0) & (src_z < NZ)
            zz = jnp.clip(src_z, 0, NZ - 1)
            part = kv_part(zz, c, grp)

            @pl.when(there)
            def _(part=part, zz=zz):
                received(part, kvup_s.at[zz, grp], kvz_r.at[zz, grp])

            if dist < NZ - 1:
                if sign < 0:
                    kv_forward(zz, grp, there & (z < NZ - 1), None)
                else:
                    kv_forward(zz, grp, None, there & (z > 0))
            send(part, part, kvsib_s.at[zz, grp], kvsib_r.at[zz, grp], sib, there)

    kv_own(0)
    kv_own(1)

    def w_block(zz, xx):
        return wbuf.at[pl.ds(pl.multiple_of((zz * 4 + xx) * 80, 80), 80)]

    @pl.when(w_core & jnp.logical_not(active & (y // 2 == four)))
    def _():
        received(w_block(z, x), wy_s.at[0], wy_r.at[0])

    for k in range(1, NZ):
        send(w_block(z, x), w_block(z, x), wz_s.at[k], wz_r.at[z], dev(z_at=(z + k) % NZ), w_core)

    def w_along_x(zz):
        for k in range(1, NX):
            send(w_block(zz, x), w_block(zz, x), wx_s.at[zz, k], wx_r.at[zz, x], dev(x_at=(x + k) % NX), w_core)

    w_along_x(z)
    kv_own(2)
    for k in range(1, NZ):
        zz = (z + k) % NZ

        @pl.when(w_core)
        def _(zz=zz):
            received(w_block(zz, x), wz_s.at[1], wz_r.at[zz])

        w_along_x(zz)

    for k in range(1, NY):
        yy = (y + k) % NY
        received(stbuf.at[yy], sty_s.at[k], sty_r.at[yy])
    y_sum = stbuf[0]
    for k in range(1, NY):
        y_sum = y_sum + stbuf[k]
    stsib[0] = y_sum
    send(stsib.at[0], stsib.at[1], stsib_s, stsib_r, sib)

    for grp in range(3):
        kv_relay(1, grp)

    received(stsib.at[1], stsib_s, stsib_r)
    stz[z] = stsib[0] + stsib[1]
    for k in range(1, NZ):
        send(stz.at[z], stz.at[z], stz_s.at[k], stz_r.at[z], dev(z_at=(z + k) % NZ))

    for grp in range(3):
        kv_relay(2, grp)

    def w_four(zz):
        return wbuf.at[pl.ds(pl.multiple_of(zz * 320, 320), 320)]

    for zz in range(NZ):
        for k in range(1, NX):
            xx = (x + k) % NX

            @pl.when(w_core)
            def _(zz=zz, xx=xx):
                received(w_block(zz, xx), wx_s.at[zz, 1], wx_r.at[zz, xx])

        send(w_four(zz), w_four(zz), ws_s.at[zz], ws_r.at[zz], sib, w_core)

    for grp in range(3):
        kv_relay(3, grp)

    for k in range(1, NZ):
        zz = (z + k) % NZ
        received(stz.at[zz], stz_s.at[k], stz_r.at[zz])
    total = stz[0]
    for k in range(1, NZ):
        total = total + stz[k]
    totals_ref[...] = total[4:8, 0:GROUPS]
    stat_rows = []
    for i in range(NY):
        own = stbuf[(y + OFF[i]) % NY]
        used = total[0:4, 0:GROUPS] - own[0:4, 0:GROUPS] + own[4:8, 0:GROUPS]
        used = jnp.where(img_b == 0, used[0:2], used[2:4])
        mean = used[0:1] / CELLS
        var = used[1:2] / CELLS - mean * mean
        stat_rows += [mean, lax.rsqrt(var + 1e-5)]
    stats = lax.dot_general(
        jnp.concatenate(stat_rows, axis=0),
        spread,
        (((1,), (0,)), ((), ())),
        precision=lax.Precision.HIGHEST,
        preferred_element_type=F32,
    )
    for i in range(NY):
        if i > 0:
            received(xbuf.at[i], x_s.at[i], x_r.at[i])
        feats = xbuf[i].astype(F32)
        normed = (feats - stats[2 * i : 2 * i + 1]) * stats[2 * i + 1 : 2 * i + 2]
        xn[i * ROWS : (i + 1) * ROWS, :] = (normed * gain_ref[...] + bias_ref[...]).astype(BF16)

    for zz in range(NZ):

        @pl.when(jnp.logical_not(w_core))
        def _(zz=zz):
            received(w_four(zz), ws_s.at[zz], ws_r.at[zz])

    fsend[...] = jnp.dot(xn[...], wbuf[:, 0:384], preferred_element_type=F32).astype(BF16).reshape(NY, ROWS, 384)
    for i in range(1, NY):
        home = (y + OFF[i]) % NY
        send(fsend.at[i], fhome.at[y], f_s.at[i], f_r.at[y], dev(y_at=home))
    fhome[y] = fsend[0]
    q_all = jnp.dot(xn[...], wbuf[:, 384:640], preferred_element_type=F32).astype(BF16).astype(F32) * 0.125
    low = lane_low((QROWS, 128))
    for s in range(UNITS):
        part = q_all[:, 0:128] if s < 2 else q_all[:, 128:256]
        if s == 1:
            part = pltpu.roll(part, HEAD_DIM, 1)
        part = jnp.where(low, part, 0.0).astype(BF16)
        qbuf[s, :, 0:128] = part
        qbuf[s, :, 128:256] = part
        kvf[s, :, 0:128] = fsend[:, :, s * 128 : s * 128 + 128].reshape(QROWS, 128)
        kvf[s, :, 128:256] = jnp.zeros((QROWS, 128), BF16)

    for zz in range(NZ):
        for grp in range(3):
            received(kv_part(zz, 1 - c, grp), kvsib_s.at[zz, grp], kvsib_r.at[zz, grp])

    low16 = lane_low((16, 128))

    def widen(step, carry):
        zc = step // NY
        slot = step % NY
        scale_tile = kv[zc // 2, zc % 2, slot, UNITS * ROWS : CHUNK, :].astype(F32)
        for t in range(3):
            factor = jnp.where(low16, scale_tile[:, 2 * t : 2 * t + 1], scale_tile[:, 2 * t + 1 : 2 * t + 2])
            for s in range(UNITS):
                code = kv[zc // 2, zc % 2, slot, s * ROWS + t * 16 : s * ROWS + t * 16 + 16, :].astype(F32)
                wide = code * factor
                high = wide.astype(BF16)
                rest = (wide - high.astype(F32)).astype(BF16)
                at = pl.ds(pl.multiple_of(slot * ROWS + t * 16, 16), 16)
                kv2[s, zc, at, 0:128] = high
                kv2[s, zc, at, 128:256] = rest
        return carry

    lax.fori_loop(0, 8 * NY, widen, 0)

    def attend(s, block, mask, first):
        scores = lax.dot_general(qbuf[s], block, (((1,), (1,)), ((), ())), preferred_element_type=F32)
        if mask is not None:
            scores = scores + mask
        top = jnp.max(scores, axis=1, keepdims=True)
        if first:
            new = jnp.broadcast_to(top, (QROWS, 128))
        else:
            old = m_ref[s]
            new = jnp.maximum(old, top)
            decay = jnp.exp(old - new)
        lifted = jnp.exp(scores - jnp.concatenate([new] * 3, axis=1))
        row_sum = lifted[:, 0:128] + lifted[:, 128:256] + lifted[:, 256:384]
        mixed = jnp.dot(lifted.astype(BF16), block, preferred_element_type=F32)
        m_ref[s] = new
        if first:
            l_ref[s] = row_sum
            acc_ref[s] = mixed
        else:
            l_ref[s] = l_ref[s] * decay + row_sum
            acc_ref[s] = acc_ref[s] * jnp.concatenate([decay, decay], axis=1) + mixed

    own_zc = z * 2 + c
    for s in range(UNITS):
        attend(s, kvf[s], mask_diag[...], True)
    for s in range(UNITS):
        attend(s, kv2[s, own_zc], mask_off[...], False)

    def others(k, carry):
        zc = (own_zc + k) % 8
        for s in range(UNITS):
            attend(s, kv2[s, zc], None, False)
        return carry

    lax.fori_loop(1, 8, others, 0)

    out = []
    for s in range(UNITS):
        total_l = jnp.sum(l_ref[s], axis=1, keepdims=True)
        out.append((acc_ref[s, :, 0:128] + acc_ref[s, :, 128:256]) / total_l)
    asend[:, :, 0:128] = join_halves(out[0], True, out[1], True).astype(BF16).reshape(NY, ROWS, 128)
    asend[:, :, 128:256] = out[2].astype(BF16).reshape(NY, ROWS, 128)
    for i in range(1, NY):
        home = (y + OFF[i]) % NY
        send(asend.at[i], ahome.at[y], a_s.at[i], a_r.at[y], dev(y_at=home))
    ahome[y] = asend[0]

    for k in range(1, NY):
        plane = (y + k) % NY
        received(fhome.at[plane], f_s.at[k], f_r.at[plane])
    for b in range(2):
        blocks = []
        for h in range(HEADS):
            g, s = (h // UNITS, h % UNITS)
            blocks.append(fhome[2 * g + b, :, s * 128 : s * 128 + 128].astype(F32))
        magnitudes = []
        for kind in range(2):
            tiles = [join_halves(blocks[2 * m], kind == 1, blocks[2 * m + 1], kind == 1) for m in range(5)]
            top = jnp.abs(tiles[0])
            for tile in tiles[1:]:
                top = jnp.maximum(top, jnp.abs(tile))
            magnitude = jnp.max(top, axis=1, keepdims=True) + 1e-06
            magnitudes.append(magnitude)
            for m in range(5):
                at = kind * 640 + m * 128
                fvals_ref[b, :, at : at + 128] = (tiles[m] / magnitude).astype(BF16)
        fscales_ref[b] = jnp.concatenate(magnitudes, axis=1).astype(BF16)

    for k in range(1, NY):
        plane = (y + k) % NY
        received(ahome.at[plane], a_s.at[k], a_r.at[plane])
    for b in range(2):
        pairs = [ahome[2 * g + b, :, 0:128].astype(F32) for g in range(4)]
        lasts = [ahome[2 * g + b, :, 128:256].astype(F32) for g in range(4)]
        att_ref[b, :, 0:128] = pairs[0].astype(BF16)
        att_ref[b, :, 128:256] = join_halves(lasts[0], True, pairs[1], False).astype(BF16)
        att_ref[b, :, 256:384] = join_halves(pairs[1], True, lasts[1], True).astype(BF16)
        att_ref[b, :, 384:512] = pairs[2].astype(BF16)
        att_ref[b, :, 512:640] = join_halves(lasts[2], True, pairs[3], False).astype(BF16)

    for finish in pending:
        finish()


def local(hidden_in, gn_gain, gn_bias, stale_local, w_qkv, stale_values, stale_scales):
    dma = pltpu.SemaphoreType.DMA
    vmem = pltpu.VMEM
    scratch = [
        vmem((NY, CHUNK, 128), BF16),
        vmem((NZ, 2, NY, CHUNK, 128), BF16),
        vmem((UNITS, 8, QROWS, 256), BF16),
        vmem((UNITS, QROWS, 256), BF16),
        vmem((NY, ROWS, D), BF16),
        vmem((QROWS, D), BF16),
        vmem((8, 128), F32),
        vmem((NY, 8, 128), F32),
        vmem((2, 8, 128), F32),
        vmem((NZ, 8, 128), F32),
        vmem((32, 1920), F32),
        vmem((4, 32, WCOLS), BF16),
        vmem((128, WCOLS), BF16),
        vmem((80, WCOLS), BF16),
        vmem((D, WCOLS), BF16),
        vmem((UNITS, QROWS, 256), BF16),
        vmem((QROWS, QROWS), F32),
        vmem((QROWS, QROWS), F32),
        vmem((UNITS, QROWS, 128), F32),
        vmem((UNITS, QROWS, 128), F32),
        vmem((UNITS, QROWS, 256), F32),
        vmem((NY, ROWS, 384), BF16),
        vmem((NY, ROWS, 384), BF16),
        vmem((NY, ROWS, 256), BF16),
        vmem((NY, ROWS, 256), BF16),
        dma((NY,)),
        dma((NY,)),
        dma((NZ, 3)),
        dma((NZ, 3)),
        dma((NZ, 3)),
        dma((NZ, 3)),
        dma((NZ, 3)),
        dma((NY,)),
        dma((NY,)),
        dma((NY,)),
        dma((NY,)),
        dma(()),
        dma(()),
        dma((NZ,)),
        dma((NZ,)),
        dma((4,)),
        dma((4,)),
        dma((2,)),
        dma((1,)),
        dma((NZ,)),
        dma((NZ,)),
        dma((NZ, NX)),
        dma((NZ, NX)),
        dma((NZ,)),
        dma((NZ,)),
        dma((NY,)),
        dma((NY,)),
        dma((NY,)),
        dma((NY,)),
    ]
    whole = pl.BlockSpec(memory_space=pltpu.VMEM)
    attended, fresh_values, fresh_scales, totals = pl.pallas_call(
        kernel,
        out_shape=(
            jax.ShapeDtypeStruct((2, ROWS, 640), BF16),
            jax.ShapeDtypeStruct((2, ROWS, D), BF16),
            jax.ShapeDtypeStruct((2, ROWS, 2), BF16),
            jax.ShapeDtypeStruct((4, GROUPS), F32),
        ),
        in_specs=[whole] * 7,
        out_specs=(whole,) * 4,
        scratch_shapes=scratch,
        compiler_params=pltpu.CompilerParams(
            collective_id=0, has_side_effects=True, vmem_limit_bytes=48 * 2**20
        ),
        name="attend_planes",
    )(
        hidden_in,
        gn_gain.reshape(1, D),
        gn_bias.reshape(1, D),
        stale_local.reshape(4, GROUPS),
        w_qkv,
        stale_values,
        stale_scales,
    )
    return attended, fresh_values, fresh_scales, totals.reshape(2, 2, GROUPS)


def solution(mesh):
    in_specs = (
        P("img", "patch", None),
        P(),
        P(),
        P("img", "patch", None, None),
        P("patch", None),
        P("img", "patch", None),
        P("img", "patch", None),
    )
    out_specs = (
        P("img", "patch", None),
        P("img", "patch", None),
        P("img", "patch", None),
        P("img", None, None),
    )
    return jax.shard_map(local, mesh=mesh, in_specs=in_specs, out_specs=out_specs, check_vma=False)
```

```python
import jax
import jax.numpy as jnp
from jax import lax
from jax.experimental import pallas as pl
from jax.experimental.pallas import tpu as pltpu
from jax.sharding import PartitionSpec as P

HEADS = 10
HEAD_DIM = 64
GROUPS = 32
D = 1280
CPG = 40
ROWS = 48
NY = 8
NZ = 4
NX = 4
QROWS = NY * ROWS
UNITS = 3
CHUNK = UNITS * ROWS + 16
WCOLS = 640
CELLS = 122880.0
KEYS = 9 * QROWS
BIG_NEG = -1e30
OFF = (0, 1, -1, 2, -2, 3, -3, 4)
KV_GROUPS = ((0, 1), (1, 2), (3, 2), (5, 3))
MESH = pl.DeviceIdType.MESH
F32 = jnp.float32
BF16 = jnp.bfloat16


def head_of(group, unit):
    return min(UNITS * group + unit, HEADS - 1)


def lane_low(shape):
    return lax.broadcasted_iota(jnp.int32, shape, 1) < HEAD_DIM


def join_halves(low, low_high, high, high_high):
    left = pltpu.roll(low, HEAD_DIM, 1) if low_high else low
    right = high if high_high else pltpu.roll(high, HEAD_DIM, 1)
    return jnp.where(lane_low(left.shape), left, right)


def kernel(
    hid_ref,
    gain_ref,
    bias_ref,
    stale_ref,
    w_ref,
    codes_ref,
    scales_ref,
    att_ref,
    fvals_ref,
    fscales_ref,
    totals_ref,
    hid,
    gain,
    bias,
    stale,
    w_own,
    codes,
    scales,
    in_sem,
    kvs,
    kv,
    kv2,
    xbuf,
    xn,
    st,
    stbuf,
    stsib,
    stz,
    w32,
    wpack,
    w0,
    w80,
    wbuf,
    qbuf,
    mask,
    fsend,
    fhome,
    asend,
    ahome,
    kvy_s,
    kvy_r,
    kvz_s,
    kvz_r,
    kvsib_s,
    kvsib_r,
    x_s,
    x_r,
    sty_s,
    sty_r,
    stsib_s,
    stsib_r,
    stz_s,
    stz_r,
    p0_s,
    p0_r,
    wy_s,
    wy_r,
    wz_s,
    wz_r,
    wx_s,
    wx_r,
    ws_s,
    ws_r,
    f_s,
    f_r,
    a_s,
    a_r,
):
    img = lax.axis_index("img")
    patch = lax.axis_index("patch")
    x = img % NX
    img_base = img - x
    z = patch // (2 * NY)
    y = (patch // 2) % NY
    c = patch % 2

    def dev(y_at=None, z_at=None, c_at=None, x_at=None):
        yy = y if y_at is None else y_at
        zz = z if z_at is None else z_at
        cc = c if c_at is None else c_at
        xx = x if x_at is None else x_at
        return {"img": img_base + xx, "patch": (zz * NY + yy) * 2 + cc}

    sib = dev(c_at=1 - c)
    y_peers = [dev(y_at=(y + k) % NY) for k in range(1, NY)]
    z_peers = [dev(z_at=(z + k) % NZ) for k in range(1, NZ)]
    x_peers = [dev(x_at=(x + k) % NX) for k in range(1, NX)]
    y_twin = y + 1 - 2 * (y % 2)
    diag = dev(y_at=y_twin, c_at=1 - c)
    everyone = y_peers + z_peers + x_peers + [sib, diag]

    barrier = pltpu.get_barrier_semaphore()
    for peer in everyone:
        pl.semaphore_signal(barrier, inc=1, device_id=peer, device_id_type=MESH)

    img_b = y % 2
    active = (y // 2) == x
    four = (y % 2) * 2 + c
    w_core = c == (y // 2) % 2

    pending = []

    def send(src, dst, s_sem, r_sem, peer, when=None):
        copy = pltpu.make_async_remote_copy(
            src_ref=src, dst_ref=dst, send_sem=s_sem, recv_sem=r_sem, device_id=peer, device_id_type=MESH
        )

        def start():
            copy.start()

        def finish():
            copy.wait_send()

        if when is None:
            start()
            pending.append(finish)
        else:
            pl.when(when)(start)
            pending.append(lambda: pl.when(when)(finish))

    def received(dst, s_sem, r_sem):
        pltpu.make_async_remote_copy(
            src_ref=dst, dst_ref=dst, send_sem=s_sem, recv_sem=r_sem, device_id=sib, device_id_type=MESH
        ).wait_recv()

    copies = []
    sources = (codes_ref, w_ref, scales_ref, hid_ref, stale_ref, gain_ref, bias_ref)
    for k, (src, dst) in enumerate(zip(sources, (codes, w_own, scales, hid, stale, gain, bias))):
        copy = pltpu.make_async_copy(src, dst, in_sem.at[k])
        copy.start()
        copies.append(copy)
    copies[1].wait()

    @pl.when(active)
    def _():
        w32[...] = jnp.zeros_like(w32)
        w32[0:20, :] = w_own[...].astype(F32)

        def piece(block, head):
            unit = block * HEADS + head
            return w32[:, (unit // 2) * 128 : (unit // 2) * 128 + 128], unit % 2 == 1

        for g in range(4):
            h = [head_of(g, s) for s in range(UNITS)]
            plan = [((1, h[s]), (2, h[s])) for s in range(UNITS)]
            plan += [((0, h[0]), (0, h[1])), ((0, h[2]), (0, h[2]))]
            for t, (first, second) in enumerate(plan):
                a, a_high = piece(*first)
                b, b_high = piece(*second)
                wpack[g, :, t * 128 : t * 128 + 128] = join_halves(a, a_high, b, b_high).astype(BF16)

    copies[0].wait()
    copies[2].wait()
    eye_row = lax.broadcasted_iota(jnp.int32, (ROWS, ROWS), 0)
    eye_col = lax.broadcasted_iota(jnp.int32, (ROWS, ROWS), 1)
    eye = jnp.where(eye_row == eye_col, 1.0, 0.0).astype(BF16)
    for b in range(2):
        lane16 = lax.broadcasted_iota(jnp.int32, (16, 128), 1)
        sc = lax.dot_general(eye, scales[b], (((1,), (1,)), ((), ())), preferred_element_type=F32)
        tile = jnp.zeros((16, 128), F32)
        for t in range(3):
            for f in range(2):
                col = sc[t * 16 : t * 16 + 16, f : f + 1]
                tile = jnp.where(lane16 == 2 * t + f, col, tile)
        tile = tile.astype(BF16)
        packed = {}
        for h in range(HEADS):
            k_tile = codes[b, :, (h // 2) * 128 : (h // 2) * 128 + 128].astype(F32)
            v_tile = codes[b, :, 640 + (h // 2) * 128 : 640 + (h // 2) * 128 + 128].astype(F32)
            odd = h % 2 == 1
            packed[h] = join_halves(k_tile, odd, v_tile, odd).astype(BF16)
        for g in range(4):
            for s in range(UNITS):
                kvs[2 * g + b, s * ROWS : (s + 1) * ROWS, :] = packed[head_of(g, s)]
            kvs[2 * g + b, UNITS * ROWS : CHUNK, :] = tile

    copies[3].wait()
    copies[4].wait()
    sub = lax.broadcasted_iota(jnp.int32, (GROUPS, D), 0) * CPG
    lane = lax.broadcasted_iota(jnp.int32, (GROUPS, D), 1)
    spread = jnp.where((lane >= sub) & (lane < sub + CPG), 1.0, 0.0).astype(F32)
    col_sums = []
    for b in range(2):
        feats = hid[b].astype(F32)
        col_sums.append(jnp.sum(feats, axis=0, keepdims=True))
        col_sums.append(jnp.sum(feats * feats, axis=0, keepdims=True))
    col_sums = jnp.concatenate(col_sums, axis=0)
    fresh = lax.dot_general(
        col_sums, spread, (((1,), (1,)), ((), ())), precision=lax.Precision.HIGHEST, preferred_element_type=F32
    )
    st[...] = jnp.zeros_like(st)
    st[0:4, 0:GROUPS] = stale[...]
    st[4:8, 0:GROUPS] = fresh
    stbuf[y] = st[...]

    kv[z, c, 0] = kvs[y]
    xbuf[0] = hid[img_b]

    pl.semaphore_wait(barrier, len(everyone))

    for j in range(4):
        peer = dev(y_at=y - y % 2 + j // 2, c_at=j % 2)
        send(wpack.at[j], w0.at[pl.ds(pl.multiple_of(four * 32, 32), 32)], p0_s.at[j], p0_r.at[four], peer, active & (four != j))

    def kv_to_plane(i):
        send(kvs.at[(y - OFF[i]) % NY], kv.at[z, c, i], kvy_s.at[i], kvy_r.at[i], dev(y_at=(y - OFF[i]) % NY))

    for i in range(1, 5):
        kv_to_plane(i)
    for k in range(1, NY):
        send(st, stbuf.at[y], sty_s.at[k], sty_r.at[y], dev(y_at=(y + k) % NY))
    def kv_part(zz, cc, grp):
        first, count = KV_GROUPS[grp]
        return kv.at[zz, cc, pl.ds(first, count)]

    def kv_own(grp):
        first, count = KV_GROUPS[grp]
        for i in range(first, first + count):
            if i > 0:
                received(kv.at[z, c, i], kvy_s.at[i], kvy_r.at[i])
        part = kv_part(z, c, grp)
        for k in range(1, NZ):
            to = (z + k) % NZ
            near = jnp.abs(to - z) < NZ - 1
            send(part, part, kvz_s.at[k, grp], kvz_r.at[z, grp], dev(z_at=to), near)
        send(part, part, kvsib_s.at[z, grp], kvsib_r.at[z, grp], sib)

    z_next = jnp.where(z == 3, 2, z + 1)
    z_other = jnp.where(z == 0, 2, jnp.where(z == 3, 1, z - 1))
    z_far = jnp.where(z < 2, 3, 0)

    def kv_arrive(grp):
        for zz in (z_next, z_other, z_far):
            part = kv_part(zz, c, grp)
            received(part, kvz_s.at[1, grp], kvz_r.at[zz, grp])
            if zz is z_far:
                middle = (z == 1) | (z == 2)
                send(part, part, kvz_s.at[0, grp], kvz_r.at[zz, grp], dev(z_at=3 - z_far), middle)
            send(part, part, kvsib_s.at[zz, grp], kvsib_r.at[zz, grp], sib)

    own_zc = z * 2 + c
    low16 = lane_low((16, 128))

    def widen(zz, cc, grp):
        place = ((zz * 2 + cc - own_zc) % 8 + 1) * QROWS
        first, count = KV_GROUPS[grp]

        def body(slot, carry):
            scale_tile = kv[zz, cc, slot, UNITS * ROWS : CHUNK, :].astype(F32)
            for t in range(3):
                factor = jnp.where(low16, scale_tile[:, 2 * t : 2 * t + 1], scale_tile[:, 2 * t + 1 : 2 * t + 2])
                at = pl.ds(pl.multiple_of(place + slot * ROWS + t * 16, 16), 16)
                for s in range(UNITS):
                    code = kv[zz, cc, slot, s * ROWS + t * 16 : s * ROWS + t * 16 + 16, :].astype(F32)
                    wide = code * factor
                    high = wide.astype(BF16)
                    kv2[s, at, 0:128] = high
                    kv2[s, at, 128:256] = (wide - high.astype(F32)).astype(BF16)
            return carry

        lax.fori_loop(first, first + count, body, 0)

    def widen_far(grp):
        for zz in (z_next, z_other, z_far):
            widen(zz, c, grp)

    def from_sibling(zz, grp):
        received(kv_part(zz, 1 - c, grp), kvsib_s.at[zz, grp], kvsib_r.at[zz, grp])
        widen(zz, 1 - c, grp)

    def from_sibling_far(grp):
        for zz in (z_next, z_other, z_far):
            from_sibling(zz, grp)

    def x_send(src, i, peer, k, when=None):
        send(src, xbuf.at[i], x_s.at[k], x_r.at[i], peer, when)

    def x_wait(i):
        received(xbuf.at[i], x_s.at[i], x_r.at[i])

    def w_block(zz, xx):
        return wbuf.at[pl.ds(pl.multiple_of((zz * 4 + xx) * 80, 80), 80)]

    def w_along_x(zz):
        for k in range(1, NX):
            send(w_block(zz, x), w_block(zz, x), wx_s.at[zz, k], wx_r.at[zz, x], dev(x_at=(x + k) % NX), w_core)

    def w_four(zz):
        return wbuf.at[pl.ds(pl.multiple_of(zz * 320, 320), 320)]

    kv_own(0)

    for i in range(NY):
        lane_q = lax.broadcasted_iota(jnp.int32, (ROWS, QROWS), 1)
        same = (lane_q >= i * ROWS) & (lane_q < (i + 1) * ROWS)
        mask[i * ROWS : (i + 1) * ROWS, 0:QROWS] = jnp.where(same, 0.0, BIG_NEG)
        mask[i * ROWS : (i + 1) * ROWS, QROWS : 2 * QROWS] = jnp.where(same, BIG_NEG, 0.0)
    copies[5].wait()
    copies[6].wait()

    w_rows = pl.ds(pl.multiple_of((z * 4 + x) * 80, 80), 80)
    for j in range(4):

        @pl.when(active & (four != j))
        def _(j=j):
            received(w0.at[pl.ds(j * 32, 32)], p0_s.at[j], p0_r.at[j])

    @pl.when(active)
    def _():
        w0[pl.ds(pl.multiple_of(four * 32, 32), 32), :] = wpack[four]
        row = lax.broadcasted_iota(jnp.int32, (80, 128), 0)
        col = lax.broadcasted_iota(jnp.int32, (80, 128), 1)
        hit = jnp.zeros((80, 128), F32)
        for a in range(4):
            hit = jnp.where((row >= 20 * a) & (row < 20 * a + 20) & (col == row + 12 * a), 1.0, hit)
        w80[...] = jnp.dot(hit.astype(BF16), w0[...], preferred_element_type=F32).astype(BF16)

    for k in range(2):
        plane = 2 * four + k

        @pl.when(active & (plane == y))
        def _():
            wbuf[w_rows, :] = w80[...]

        send(w80, wbuf.at[w_rows], wy_s.at[k], wy_r.at[0], dev(y_at=plane), active & (plane != y))

    for i in range(5, NY):
        kv_to_plane(i)
    kv_own(1)
    for i in range(1, 5):
        dest = (y - OFF[i]) % NY
        x_send(hid.at[dest % 2], i, dev(y_at=dest), i)

    @pl.when(w_core & jnp.logical_not(active & (y // 2 == four)))
    def _():
        received(w_block(z, x), wy_s.at[0], wy_r.at[0])

    for k in range(1, NZ):
        send(w_block(z, x), w_block(z, x), wz_s.at[k], wz_r.at[z], dev(z_at=(z + k) % NZ), w_core)
    w_along_x(z)
    kv_own(2)
    kv_arrive(0)

    for k in range(1, NY):
        yy = (y + k) % NY
        received(stbuf.at[yy], sty_s.at[k], sty_r.at[yy])
    y_sum = stbuf[0]
    for k in range(1, NY):
        y_sum = y_sum + stbuf[k]
    stsib[0] = y_sum
    send(stsib.at[0], stsib.at[1], stsib_s, stsib_r, sib)

    for zz in (z_next, z_other, z_far):

        @pl.when(w_core)
        def _(zz=zz):
            received(w_block(zz, x), wz_s.at[1], wz_r.at[zz])

        w_along_x(zz)
    kv_own(3)

    received(stsib.at[1], stsib_s, stsib_r)
    stz[z] = stsib[0] + stsib[1]
    for k in range(1, NZ):
        send(stz.at[z], stz.at[z], stz_s.at[k], stz_r.at[z], dev(z_at=(z + k) % NZ))

    for i in (1, 2):
        x_wait(i)
        x_send(xbuf.at[i], 4 + i, dev(y_at=(y - 2 * OFF[i]) % NY), 4 + i)
    kv_arrive(1)
    for grp in range(4):
        widen(z, c, grp)
    for i, core in ((3, 0), (4, 1)):
        x_wait(i)
        x_send(xbuf.at[i], 7, dev(y_at=(y - OFF[i]) % NY), 7 + core, c == core)
    kv_arrive(2)
    for grp in range(4):
        from_sibling(z, grp)

    for zz in range(NZ):
        for k in range(1, NX):
            xx = (x + k) % NX

            @pl.when(w_core)
            def _(zz=zz, xx=xx):
                received(w_block(zz, xx), wx_s.at[zz, 1], wx_r.at[zz, xx])

        send(w_four(zz), w_four(zz), ws_s.at[zz], ws_r.at[zz], sib, w_core)
    for grp in range(3):
        widen_far(grp)
        from_sibling_far(grp)
    kv_arrive(3)

    for k in range(1, NZ):
        zz = (z + k) % NZ
        received(stz.at[zz], stz_s.at[k], stz_r.at[zz])
    total = stz[0]
    for k in range(1, NZ):
        total = total + stz[k]
    totals_ref[...] = total[4:8, 0:GROUPS]
    stat_rows = []
    for i in range(NY):
        own = stbuf[(y + OFF[i]) % NY]
        used = total[0:4, 0:GROUPS] - own[0:4, 0:GROUPS] + own[4:8, 0:GROUPS]
        used = jnp.where(img_b == 0, used[0:2], used[2:4])
        mean = used[0:1] / CELLS
        var = used[1:2] / CELLS - mean * mean
        stat_rows += [mean, lax.rsqrt(var + 1e-5)]
    stats = lax.dot_general(
        jnp.concatenate(stat_rows, axis=0),
        spread,
        (((1,), (0,)), ((), ())),
        precision=lax.Precision.HIGHEST,
        preferred_element_type=F32,
    )
    gain_row = gain[...].reshape(1, D)
    bias_row = bias[...].reshape(1, D)
    for i in range(NY):
        if i > 4:
            x_wait(i)
        feats = xbuf[i].astype(F32)
        normed = (feats - stats[2 * i : 2 * i + 1]) * stats[2 * i + 1 : 2 * i + 2]
        xn[i * ROWS : (i + 1) * ROWS, :] = (normed * gain_row + bias_row).astype(BF16)

    for zz in range(NZ):

        @pl.when(jnp.logical_not(w_core))
        def _(zz=zz):
            received(w_four(zz), ws_s.at[zz], ws_r.at[zz])

    fsend[...] = jnp.dot(xn[...], wbuf[:, 0:384], preferred_element_type=F32).astype(BF16).reshape(NY, ROWS, 384)
    for i in range(1, NY):
        home = (y + OFF[i]) % NY
        send(fsend.at[i], fhome.at[y], f_s.at[i], f_r.at[y], dev(y_at=home))
    fhome[y] = fsend[0]
    q_all = jnp.dot(xn[...], wbuf[:, 384:640], preferred_element_type=F32).astype(BF16).astype(F32) * 0.125
    low = lane_low((QROWS, 128))
    for s in range(UNITS):
        part = q_all[:, 0:128] if s < 2 else q_all[:, 128:256]
        if s == 1:
            part = pltpu.roll(part, HEAD_DIM, 1)
        part = jnp.where(low, part, 0.0).astype(BF16)
        qbuf[s, :, 0:128] = part
        qbuf[s, :, 128:256] = part
        kv2[s, 0:QROWS, 0:128] = fsend[:, :, s * 128 : s * 128 + 128].reshape(QROWS, 128)
        kv2[s, 0:QROWS, 128:256] = jnp.zeros((QROWS, 128), BF16)

    widen_far(3)
    from_sibling_far(3)

    jobs = [(s, at, min(2 * QROWS, KEYS - at)) for s in range(UNITS) for at in range(0, KEYS, 2 * QROWS)]

    def scores_of(s, at, size):
        found = lax.dot_general(
            qbuf[s], kv2[s, at : at + size, :], (((1,), (1,)), ((), ())), preferred_element_type=F32
        )
        return found + mask[...] if at == 0 else found

    def go_home(k):
        for i in range(1, NY):
            home = (y + OFF[i]) % NY
            send(asend.at[k, i], ahome.at[k, y], a_s.at[k, i], a_r.at[k, y], dev(y_at=home))
        ahome[k, y] = asend[k, 0]

    upcoming = scores_of(*jobs[0])
    out = []
    for n, (s, at, size) in enumerate(jobs):
        scores = upcoming
        if n + 1 < len(jobs):
            upcoming = scores_of(*jobs[n + 1])
        top = jnp.max(scores, axis=1, keepdims=True)
        if at == 0:
            new = jnp.broadcast_to(top, (QROWS, 128))
        else:
            new = jnp.maximum(old, top)
            decay = jnp.exp(old - new)
        lifted = jnp.exp(scores - jnp.concatenate([new] * (size // 128), axis=1))
        row_sum = lifted[:, 0:128]
        for k in range(1, size // 128):
            row_sum = row_sum + lifted[:, k * 128 : k * 128 + 128]
        mixed = jnp.dot(lifted.astype(BF16), kv2[s, at : at + size, :], preferred_element_type=F32)
        if at > 0:
            row_sum = running * decay + row_sum
            mixed = acc * jnp.concatenate([decay, decay], axis=1) + mixed
        old, running, acc = new, row_sum, mixed
        if at + size == KEYS:
            out.append((acc[:, 0:128] + acc[:, 128:256]) / jnp.sum(running, axis=1, keepdims=True))
            if s == 1:
                asend[0] = join_halves(out[0], True, out[1], True).astype(BF16).reshape(NY, ROWS, 128)
                go_home(0)
    asend[1] = out[2].astype(BF16).reshape(NY, ROWS, 128)
    go_home(1)

    for k in range(1, NY):
        plane = (y + k) % NY
        received(fhome.at[plane], f_s.at[k], f_r.at[plane])
    for b in range(2):
        blocks = []
        for h in range(HEADS):
            g, s = (h // UNITS, h % UNITS)
            blocks.append(fhome[2 * g + b, :, s * 128 : s * 128 + 128].astype(F32))
        magnitudes = []
        for kind in range(2):
            tiles = [join_halves(blocks[2 * m], kind == 1, blocks[2 * m + 1], kind == 1) for m in range(5)]
            top = jnp.abs(tiles[0])
            for tile in tiles[1:]:
                top = jnp.maximum(top, jnp.abs(tile))
            magnitude = jnp.max(top, axis=1, keepdims=True) + 1e-06
            magnitudes.append(magnitude)
            for m in range(5):
                at = kind * 640 + m * 128
                fvals_ref[b, :, at : at + 128] = (tiles[m] / magnitude).astype(BF16)
        both = jnp.concatenate(magnitudes, axis=1).astype(BF16)
        turned = lax.dot_general(both, eye, (((0,), (0,)), ((), ())), preferred_element_type=F32)
        fscales_ref[b] = turned.astype(BF16)

    for part in range(2):
        for k in range(1, NY):
            plane = (y + k) % NY
            received(ahome.at[part, plane], a_s.at[part, k], a_r.at[part, plane])
    for b in range(2):
        pairs = [ahome[0, 2 * g + b].astype(F32) for g in range(4)]
        lasts = [ahome[1, 2 * g + b].astype(F32) for g in range(4)]
        att_ref[b, :, 0:128] = pairs[0].astype(BF16)
        att_ref[b, :, 128:256] = join_halves(lasts[0], True, pairs[1], False).astype(BF16)
        att_ref[b, :, 256:384] = join_halves(pairs[1], True, lasts[1], True).astype(BF16)
        att_ref[b, :, 384:512] = pairs[2].astype(BF16)
        att_ref[b, :, 512:640] = join_halves(lasts[2], True, pairs[3], False).astype(BF16)

    for finish in pending:
        finish()


def write_out(a, b, c, d, a_out, b_out, c_out, d_out, a_mid, b_mid, c_mid, d_mid, sems):
    mids = (a_mid, b_mid, c_mid, d_mid)
    steps = []
    for k, src in enumerate((a, b, c, d)):
        steps.append(pltpu.make_async_copy(src, mids[k], sems.at[k]))
        steps[k].start()
    out = []
    for k, dst in enumerate((a_out, b_out, c_out, d_out)):
        steps[k].wait()
        out.append(pltpu.make_async_copy(mids[k], dst, sems.at[4 + k]))
        out[k].start()
    for copy in out:
        copy.wait()


def local(hidden_in, gn_gain, gn_bias, stale_local, w_qkv, stale_values, stale_scales):
    dma = pltpu.SemaphoreType.DMA
    vmem = pltpu.VMEM
    scratch = [
        vmem((2, ROWS, D), BF16),
        vmem((D,), F32),
        vmem((D,), F32),
        vmem((4, GROUPS), F32),
        vmem((20, 1920), BF16),
        vmem((2, ROWS, D), BF16),
        vmem((2, 2, ROWS), BF16),
        dma((7,)),
        vmem((NY, CHUNK, 128), BF16),
        vmem((NZ, 2, NY, CHUNK, 128), BF16),
        vmem((UNITS, KEYS, 256), BF16),
        vmem((NY, ROWS, D), BF16),
        vmem((QROWS, D), BF16),
        vmem((8, 128), F32),
        vmem((NY, 8, 128), F32),
        vmem((2, 8, 128), F32),
        vmem((NZ, 8, 128), F32),
        vmem((32, 1920), F32),
        vmem((4, 32, WCOLS), BF16),
        vmem((128, WCOLS), BF16),
        vmem((80, WCOLS), BF16),
        vmem((D, WCOLS), BF16),
        vmem((UNITS, QROWS, 256), BF16),
        vmem((QROWS, 2 * QROWS), F32),
        vmem((NY, ROWS, 384), BF16),
        vmem((NY, ROWS, 384), BF16),
        vmem((2, NY, ROWS, 128), BF16),
        vmem((2, NY, ROWS, 128), BF16),
        dma((NY,)),
        dma((NY,)),
        dma((NZ, 4)),
        dma((NZ, 4)),
        dma((NZ, 4)),
        dma((NZ, 4)),
        dma((NY + 1,)),
        dma((NY,)),
        dma((NY,)),
        dma((NY,)),
        dma(()),
        dma(()),
        dma((NZ,)),
        dma((NZ,)),
        dma((4,)),
        dma((4,)),
        dma((2,)),
        dma((1,)),
        dma((NZ,)),
        dma((NZ,)),
        dma((NZ, NX)),
        dma((NZ, NX)),
        dma((NZ,)),
        dma((NZ,)),
        dma((NY,)),
        dma((NY,)),
        dma((2, NY)),
        dma((2, NY)),
    ]
    whole = pl.BlockSpec(memory_space=pltpu.VMEM)
    anywhere = pl.BlockSpec(memory_space=pl.ANY)
    out_shape = (
        jax.ShapeDtypeStruct((2, ROWS, 640), BF16),
        jax.ShapeDtypeStruct((2, ROWS, D), BF16),
        jax.ShapeDtypeStruct((2, 2, ROWS), BF16),
        jax.ShapeDtypeStruct((4, GROUPS), F32),
    )
    results = pl.pallas_call(
        kernel,
        out_shape=out_shape,
        in_specs=[anywhere] * 7,
        out_specs=(whole,) * 4,
        scratch_shapes=scratch,
        compiler_params=pltpu.CompilerParams(
            collective_id=0, has_side_effects=True, vmem_limit_bytes=56 * 2**20
        ),
        name="attend_planes",
    )(
        hidden_in,
        gn_gain,
        gn_bias,
        stale_local.reshape(4, GROUPS),
        w_qkv,
        stale_values,
        jnp.transpose(stale_scales, (0, 2, 1)),
    )
    attended, fresh_values, fresh_scales, totals = pl.pallas_call(
        write_out,
        out_shape=out_shape,
        in_specs=[anywhere] * 4,
        out_specs=(anywhere,) * 4,
        scratch_shapes=[vmem(o.shape, o.dtype) for o in out_shape] + [dma((8,))],
        compiler_params=pltpu.CompilerParams(vmem_limit_bytes=62 * 2**20),
        name="write_out",
    )(*results)
    return attended, fresh_values, jnp.transpose(fresh_scales, (0, 2, 1)), totals.reshape(2, 2, GROUPS)


def solution(mesh):
    in_specs = (
        P("img", "patch", None),
        P(),
        P(),
        P("img", "patch", None, None),
        P("patch", None),
        P("img", "patch", None),
        P("img", "patch", None),
    )
    out_specs = (
        P("img", "patch", None),
        P("img", "patch", None),
        P("img", "patch", None),
        P("img", None, None),
    )
    return jax.shard_map(local, mesh=mesh, in_specs=in_specs, out_specs=out_specs, check_vma=False)
```

```python
import jax
import jax.numpy as jnp
from jax import lax
from jax.experimental import pallas as pl
from jax.experimental.pallas import tpu as pltpu
from jax.sharding import PartitionSpec as P

HEADS = 10
HEAD_DIM = 64
GROUPS = 32
D = 1280
CPG = 40
ROWS = 48
NY = 8
NZ = 4
NX = 4
QROWS = NY * ROWS
UNITS = 3
CHUNK = UNITS * ROWS + 16
WCOLS = 640
CELLS = 122880.0
KEYS = 9 * QROWS
BIG_NEG = -1e30
OFF = (0, 1, -1, 2, -2, 3, -3, 4)
KV_GROUPS = ((0, 1), (1, 2), (3, 2), (5, 3))
MESH = pl.DeviceIdType.MESH
F32 = jnp.float32
BF16 = jnp.bfloat16


def head_of(group, unit):
    return min(UNITS * group + unit, HEADS - 1)


def lane_low(shape):
    return lax.broadcasted_iota(jnp.int32, shape, 1) < HEAD_DIM


def join_halves(low, low_high, high, high_high):
    left = pltpu.roll(low, HEAD_DIM, 1) if low_high else low
    right = high if high_high else pltpu.roll(high, HEAD_DIM, 1)
    return jnp.where(lane_low(left.shape), left, right)


def kernel(
    hid_ref,
    gain_ref,
    bias_ref,
    stale_ref,
    w_ref,
    codes_ref,
    scales_ref,
    att_ref,
    fvals_ref,
    fscales_ref,
    totals_ref,
    hid,
    gain,
    bias,
    stale,
    w_own,
    codes,
    scales,
    in_sem,
    kvs,
    kv,
    kv2,
    xbuf,
    xn,
    st,
    stbuf,
    stsib,
    stz,
    w32,
    wpack,
    w0,
    w80,
    wbuf,
    qbuf,
    mask,
    fsend,
    fhome,
    asend,
    ahome,
    kvy_s,
    kvy_r,
    kvz_s,
    kvz_r,
    kvsib_s,
    kvsib_r,
    x_s,
    x_r,
    sty_s,
    sty_r,
    stsib_s,
    stsib_r,
    stz_s,
    stz_r,
    p0_s,
    p0_r,
    wy_s,
    wy_r,
    wz_s,
    wz_r,
    wx_s,
    wx_r,
    ws_s,
    ws_r,
    f_s,
    f_r,
    a_s,
    a_r,
):
    img = lax.axis_index("img")
    patch = lax.axis_index("patch")
    x = img % NX
    img_base = img - x
    z = patch // (2 * NY)
    y = (patch // 2) % NY
    c = patch % 2

    def dev(y_at=None, z_at=None, c_at=None, x_at=None):
        yy = y if y_at is None else y_at
        zz = z if z_at is None else z_at
        cc = c if c_at is None else c_at
        xx = x if x_at is None else x_at
        return {"img": img_base + xx, "patch": (zz * NY + yy) * 2 + cc}

    sib = dev(c_at=1 - c)
    y_peers = [dev(y_at=(y + k) % NY) for k in range(1, NY)]
    z_peers = [dev(z_at=(z + k) % NZ) for k in range(1, NZ)]
    x_peers = [dev(x_at=(x + k) % NX) for k in range(1, NX)]
    ring = (img // NX) * NZ + z

    def on_ring(step):
        at = (ring + step) % (2 * NZ)
        return {"img": (at // NZ) * NX + x, "patch": ((at % NZ) * NY + y) * 2 + c}

    ring_peers = [on_ring(step) for step in (1, -1, 2, -2)]
    y_twin = y + 1 - 2 * (y % 2)
    diag = dev(y_at=y_twin, c_at=1 - c)
    everyone = y_peers + z_peers + x_peers + ring_peers + [sib, diag]

    barrier = pltpu.get_barrier_semaphore()
    for peer in everyone:
        pl.semaphore_signal(barrier, inc=1, device_id=peer, device_id_type=MESH)

    img_b = y % 2
    active = (y // 2) == x
    four = (y % 2) * 2 + c
    w_core = c == (y // 2) % 2

    pending = []

    def send(src, dst, s_sem, r_sem, peer, when=None):
        copy = pltpu.make_async_remote_copy(
            src_ref=src, dst_ref=dst, send_sem=s_sem, recv_sem=r_sem, device_id=peer, device_id_type=MESH
        )

        def start():
            copy.start()

        def finish():
            copy.wait_send()

        if when is None:
            start()
            pending.append(finish)
        else:
            pl.when(when)(start)
            pending.append(lambda: pl.when(when)(finish))

    def received(dst, s_sem, r_sem):
        pltpu.make_async_remote_copy(
            src_ref=dst, dst_ref=dst, send_sem=s_sem, recv_sem=r_sem, device_id=sib, device_id_type=MESH
        ).wait_recv()

    copies = []
    sources = (codes_ref, w_ref, scales_ref, hid_ref, stale_ref, gain_ref, bias_ref)
    for k, (src, dst) in enumerate(zip(sources, (codes, w_own, scales, hid, stale, gain, bias))):
        copy = pltpu.make_async_copy(src, dst, in_sem.at[k])
        copy.start()
        copies.append(copy)
    copies[1].wait()

    @pl.when(active)
    def _():
        w32[...] = jnp.zeros_like(w32)
        w32[0:20, :] = w_own[...].astype(F32)

        def piece(block, head):
            unit = block * HEADS + head
            return w32[:, (unit // 2) * 128 : (unit // 2) * 128 + 128], unit % 2 == 1

        for g in range(4):
            h = [head_of(g, s) for s in range(UNITS)]
            plan = [((1, h[s]), (2, h[s])) for s in range(UNITS)]
            plan += [((0, h[0]), (0, h[1])), ((0, h[2]), (0, h[2]))]
            for t, (first, second) in enumerate(plan):
                a, a_high = piece(*first)
                b, b_high = piece(*second)
                wpack[g, :, t * 128 : t * 128 + 128] = join_halves(a, a_high, b, b_high).astype(BF16)

    copies[0].wait()
    copies[2].wait()
    eye_row = lax.broadcasted_iota(jnp.int32, (ROWS, ROWS), 0)
    eye_col = lax.broadcasted_iota(jnp.int32, (ROWS, ROWS), 1)
    eye = jnp.where(eye_row == eye_col, 1.0, 0.0).astype(BF16)
    for b in range(2):
        lane16 = lax.broadcasted_iota(jnp.int32, (16, 128), 1)
        sc = lax.dot_general(eye, scales[b], (((1,), (1,)), ((), ())), preferred_element_type=F32)
        tile = jnp.zeros((16, 128), F32)
        for t in range(3):
            for f in range(2):
                col = sc[t * 16 : t * 16 + 16, f : f + 1]
                tile = jnp.where(lane16 == 2 * t + f, col, tile)
        tile = tile.astype(BF16)
        packed = {}
        for h in range(HEADS):
            k_tile = codes[b, :, (h // 2) * 128 : (h // 2) * 128 + 128].astype(F32)
            v_tile = codes[b, :, 640 + (h // 2) * 128 : 640 + (h // 2) * 128 + 128].astype(F32)
            odd = h % 2 == 1
            packed[h] = join_halves(k_tile, odd, v_tile, odd).astype(BF16)
        for g in range(4):
            for s in range(UNITS):
                kvs[2 * g + b, s * ROWS : (s + 1) * ROWS, :] = packed[head_of(g, s)]
            kvs[2 * g + b, UNITS * ROWS : CHUNK, :] = tile

    copies[3].wait()
    copies[4].wait()
    sub = lax.broadcasted_iota(jnp.int32, (GROUPS, D), 0) * CPG
    lane = lax.broadcasted_iota(jnp.int32, (GROUPS, D), 1)
    spread = jnp.where((lane >= sub) & (lane < sub + CPG), 1.0, 0.0).astype(F32)
    col_sums = []
    for b in range(2):
        feats = hid[b].astype(F32)
        col_sums.append(jnp.sum(feats, axis=0, keepdims=True))
        col_sums.append(jnp.sum(feats * feats, axis=0, keepdims=True))
    col_sums = jnp.concatenate(col_sums, axis=0)
    fresh = lax.dot_general(
        col_sums, spread, (((1,), (1,)), ((), ())), precision=lax.Precision.HIGHEST, preferred_element_type=F32
    )
    st[...] = jnp.zeros_like(st)
    st[0:4, 0:GROUPS] = stale[...]
    st[4:8, 0:GROUPS] = fresh
    stbuf[y] = st[...]

    kv[z, c, 0] = kvs[y]
    xbuf[0] = hid[img_b]

    pl.semaphore_wait(barrier, len(everyone))

    for j in range(4):
        peer = dev(y_at=y - y % 2 + j // 2, c_at=j % 2)
        send(wpack.at[j], w0.at[pl.ds(pl.multiple_of(four * 32, 32), 32)], p0_s.at[j], p0_r.at[four], peer, active & (four != j))

    def kv_to_plane(i):
        send(kvs.at[(y - OFF[i]) % NY], kv.at[z, c, i], kvy_s.at[i], kvy_r.at[i], dev(y_at=(y - OFF[i]) % NY))

    for i in range(1, 5):
        kv_to_plane(i)
    for k in range(1, NY):
        send(st, stbuf.at[y], sty_s.at[k], sty_r.at[y], dev(y_at=(y + k) % NY))
    def kv_part(zz, cc, grp):
        first, count = KV_GROUPS[grp]
        return kv.at[zz, cc, pl.ds(first, count)]

    def kv_own(grp):
        first, count = KV_GROUPS[grp]
        for i in range(first, first + count):
            if i > 0:
                received(kv.at[z, c, i], kvy_s.at[i], kvy_r.at[i])
        part = kv_part(z, c, grp)
        for k in range(1, NZ):
            to = (z + k) % NZ
            near = jnp.abs(to - z) < NZ - 1
            send(part, part, kvz_s.at[k, grp], kvz_r.at[z, grp], dev(z_at=to), near)
        send(part, part, kvsib_s.at[z, grp], kvsib_r.at[z, grp], sib)

    z_next = jnp.where(z == 3, 2, z + 1)
    z_other = jnp.where(z == 0, 2, jnp.where(z == 3, 1, z - 1))
    z_far = jnp.where(z < 2, 3, 0)

    def kv_arrive(grp):
        for zz in (z_next, z_other, z_far):
            part = kv_part(zz, c, grp)
            received(part, kvz_s.at[1, grp], kvz_r.at[zz, grp])
            if zz is z_far:
                middle = (z == 1) | (z == 2)
                send(part, part, kvz_s.at[0, grp], kvz_r.at[zz, grp], dev(z_at=3 - z_far), middle)
            send(part, part, kvsib_s.at[zz, grp], kvsib_r.at[zz, grp], sib)

    own_zc = z * 2 + c
    low16 = lane_low((16, 128))

    def widen(zz, cc, grp):
        place = ((zz * 2 + cc - own_zc) % 8 + 1) * QROWS
        first, count = KV_GROUPS[grp]

        def body(slot, carry):
            scale_tile = kv[zz, cc, slot, UNITS * ROWS : CHUNK, :].astype(F32)
            for t in range(3):
                factor = jnp.where(low16, scale_tile[:, 2 * t : 2 * t + 1], scale_tile[:, 2 * t + 1 : 2 * t + 2])
                at = pl.ds(pl.multiple_of(place + slot * ROWS + t * 16, 16), 16)
                for s in range(UNITS):
                    code = kv[zz, cc, slot, s * ROWS + t * 16 : s * ROWS + t * 16 + 16, :].astype(F32)
                    wide = code * factor
                    high = wide.astype(BF16)
                    kv2[s, at, 0:128] = high
                    kv2[s, at, 128:256] = (wide - high.astype(F32)).astype(BF16)
            return carry

        lax.fori_loop(first, first + count, body, 0)

    def widen_far(grp):
        for zz in (z_next, z_other, z_far):
            widen(zz, c, grp)

    def from_sibling(zz, grp):
        received(kv_part(zz, 1 - c, grp), kvsib_s.at[zz, grp], kvsib_r.at[zz, grp])
        widen(zz, 1 - c, grp)

    def from_sibling_far(grp):
        for zz in (z_next, z_other, z_far):
            from_sibling(zz, grp)

    def x_send(src, i, peer, k, when=None):
        send(src, xbuf.at[i], x_s.at[k], x_r.at[i], peer, when)

    def x_wait(i):
        received(xbuf.at[i], x_s.at[i], x_r.at[i])

    def w_block(zz, xx):
        return wbuf.at[pl.ds(pl.multiple_of((zz * 4 + xx) * 80, 80), 80)]

    def w_along_x(zz):
        for k in range(1, NX):
            send(w_block(zz, x), w_block(zz, x), wx_s.at[zz, k], wx_r.at[zz, x], dev(x_at=(x + k) % NX), w_core)

    def w_four(zz):
        return wbuf.at[pl.ds(pl.multiple_of(zz * 320, 320), 320)]

    kv_own(0)

    for i in range(NY):
        lane_q = lax.broadcasted_iota(jnp.int32, (ROWS, QROWS), 1)
        same = (lane_q >= i * ROWS) & (lane_q < (i + 1) * ROWS)
        mask[i * ROWS : (i + 1) * ROWS, 0:QROWS] = jnp.where(same, 0.0, BIG_NEG)
        mask[i * ROWS : (i + 1) * ROWS, QROWS : 2 * QROWS] = jnp.where(same, BIG_NEG, 0.0)
    copies[5].wait()
    copies[6].wait()

    w_rows = pl.ds(pl.multiple_of((z * 4 + x) * 80, 80), 80)
    for j in range(4):

        @pl.when(active & (four != j))
        def _(j=j):
            received(w0.at[pl.ds(j * 32, 32)], p0_s.at[j], p0_r.at[j])

    @pl.when(active)
    def _():
        w0[pl.ds(pl.multiple_of(four * 32, 32), 32), :] = wpack[four]
        row = lax.broadcasted_iota(jnp.int32, (80, 128), 0)
        col = lax.broadcasted_iota(jnp.int32, (80, 128), 1)
        hit = jnp.zeros((80, 128), F32)
        for a in range(4):
            hit = jnp.where((row >= 20 * a) & (row < 20 * a + 20) & (col == row + 12 * a), 1.0, hit)
        w80[...] = jnp.dot(hit.astype(BF16), w0[...], preferred_element_type=F32).astype(BF16)

    for k in range(2):
        plane = 2 * four + k

        @pl.when(active & (plane == y))
        def _():
            wbuf[w_rows, :] = w80[...]

        send(w80, wbuf.at[w_rows], wy_s.at[k], wy_r.at[0], dev(y_at=plane), active & (plane != y))

    kv_own(1)

    for k in range(1, NY):
        yy = (y + k) % NY
        received(stbuf.at[yy], sty_s.at[k], sty_r.at[yy])
    y_sum = stbuf[0]
    for k in range(1, NY):
        y_sum = y_sum + stbuf[k]
    stsib[0] = y_sum
    send(stsib.at[0], stsib.at[1], stsib_s, stsib_r, sib)


    @pl.when(w_core & jnp.logical_not(active & (y // 2 == four)))
    def _():
        received(w_block(z, x), wy_s.at[0], wy_r.at[0])

    def w_rows_of(zz, first, count):
        return wbuf.at[pl.ds(pl.multiple_of((zz * 4 + x) * 80 + first, 16), count)]

    ring_parts = ((1, 0, 80), (-1, 0, 80), (2, 0, 48), (-2, 48, 32))
    for n, (step, first, count) in enumerate(ring_parts):
        mine = w_rows_of(z, first, count)
        send(mine, mine, wz_s.at[n], wz_r.at[n], on_ring(step), w_core)
    w_along_x(z)

    for i in range(5, NY):
        kv_to_plane(i)

    kv_own(2)

    for i in range(1, 5):
        dest = (y - OFF[i]) % NY
        x_send(hid.at[dest % 2], i, dev(y_at=dest), i)


    kv_arrive(0)

    for n, (step, first, count) in enumerate(ring_parts):
        zz = (z - step) % NZ

        @pl.when(w_core)
        def _(n=n, zz=zz, first=first, count=count):
            received(w_rows_of(zz, first, count), wz_s.at[n], wz_r.at[n])

        if n != 2:
            w_along_x(zz)

    kv_own(3)

    received(stsib.at[1], stsib_s, stsib_r)
    stz[z] = stsib[0] + stsib[1]
    for k in range(1, NZ):
        send(stz.at[z], stz.at[z], stz_s.at[k], stz_r.at[z], dev(z_at=(z + k) % NZ))


    for i in (1, 2):
        x_wait(i)
        x_send(xbuf.at[i], 4 + i, dev(y_at=(y - 2 * OFF[i]) % NY), 4 + i)

    kv_arrive(1)

    for grp in range(4):
        widen(z, c, grp)

    for i, core in ((3, 0), (4, 1)):
        x_wait(i)
        x_send(xbuf.at[i], 7, dev(y_at=(y - OFF[i]) % NY), 7 + core, c == core)

    kv_arrive(2)
    for grp in range(4):
        from_sibling(z, grp)

    for zz in range(NZ):
        for k in range(1, NX):
            xx = (x + k) % NX

            @pl.when(w_core)
            def _(zz=zz, xx=xx):
                received(w_block(zz, xx), wx_s.at[zz, 1], wx_r.at[zz, xx])

        send(w_four(zz), w_four(zz), ws_s.at[zz], ws_r.at[zz], sib, w_core)
    for grp in range(3):
        widen_far(grp)
        from_sibling_far(grp)
    kv_arrive(3)

    for k in range(1, NZ):
        zz = (z + k) % NZ
        received(stz.at[zz], stz_s.at[k], stz_r.at[zz])
    total = stz[0]
    for k in range(1, NZ):
        total = total + stz[k]
    totals_ref[...] = total[4:8, 0:GROUPS]
    stat_rows = []
    for i in range(NY):
        own = stbuf[(y + OFF[i]) % NY]
        used = total[0:4, 0:GROUPS] - own[0:4, 0:GROUPS] + own[4:8, 0:GROUPS]
        used = jnp.where(img_b == 0, used[0:2], used[2:4])
        mean = used[0:1] / CELLS
        var = used[1:2] / CELLS - mean * mean
        stat_rows += [mean, lax.rsqrt(var + 1e-5)]
    stats = lax.dot_general(
        jnp.concatenate(stat_rows, axis=0),
        spread,
        (((1,), (0,)), ((), ())),
        precision=lax.Precision.HIGHEST,
        preferred_element_type=F32,
    )
    gain_row = gain[...].reshape(1, D)
    bias_row = bias[...].reshape(1, D)
    for i in range(NY):
        if i > 4:
            x_wait(i)
        feats = xbuf[i].astype(F32)
        normed = (feats - stats[2 * i : 2 * i + 1]) * stats[2 * i + 1 : 2 * i + 2]
        xn[i * ROWS : (i + 1) * ROWS, :] = (normed * gain_row + bias_row).astype(BF16)

    for zz in range(NZ):

        @pl.when(jnp.logical_not(w_core))
        def _(zz=zz):
            received(w_four(zz), ws_s.at[zz], ws_r.at[zz])

    fsend[...] = jnp.dot(xn[...], wbuf[:, 0:384], preferred_element_type=F32).astype(BF16).reshape(NY, ROWS, 384)
    for i in range(1, NY):
        home = (y + OFF[i]) % NY
        send(fsend.at[i], fhome.at[y], f_s.at[i], f_r.at[y], dev(y_at=home))
    fhome[y] = fsend[0]
    q_all = jnp.dot(xn[...], wbuf[:, 384:640], preferred_element_type=F32).astype(BF16).astype(F32) * 0.125
    low = lane_low((QROWS, 128))
    for s in range(UNITS):
        part = q_all[:, 0:128] if s < 2 else q_all[:, 128:256]
        if s == 1:
            part = pltpu.roll(part, HEAD_DIM, 1)
        part = jnp.where(low, part, 0.0).astype(BF16)
        qbuf[s, :, 0:128] = part
        qbuf[s, :, 128:256] = part
        kv2[s, 0:QROWS, 0:128] = fsend[:, :, s * 128 : s * 128 + 128].reshape(QROWS, 128)
        kv2[s, 0:QROWS, 128:256] = jnp.zeros((QROWS, 128), BF16)

    widen_far(3)
    from_sibling_far(3)

    jobs = [(s, at, min(2 * QROWS, KEYS - at)) for s in range(UNITS) for at in range(0, KEYS, 2 * QROWS)]

    def scores_of(s, at, size):
        found = lax.dot_general(
            qbuf[s], kv2[s, at : at + size, :], (((1,), (1,)), ((), ())), preferred_element_type=F32
        )
        return found + mask[...] if at == 0 else found

    def go_home(k):
        for i in range(1, NY):
            home = (y + OFF[i]) % NY
            send(asend.at[k, i], ahome.at[k, y], a_s.at[k, i], a_r.at[k, y], dev(y_at=home))
        ahome[k, y] = asend[k, 0]

    upcoming = scores_of(*jobs[0])
    out = []
    for n, (s, at, size) in enumerate(jobs):
        scores = upcoming
        if n + 1 < len(jobs):
            upcoming = scores_of(*jobs[n + 1])
        top = jnp.max(scores, axis=1, keepdims=True)
        if at == 0:
            new = jnp.broadcast_to(top, (QROWS, 128))
        else:
            new = jnp.maximum(old, top)
            decay = jnp.exp(old - new)
        lifted = jnp.exp(scores - jnp.concatenate([new] * (size // 128), axis=1))
        row_sum = lifted[:, 0:128]
        for k in range(1, size // 128):
            row_sum = row_sum + lifted[:, k * 128 : k * 128 + 128]
        mixed = jnp.dot(lifted.astype(BF16), kv2[s, at : at + size, :], preferred_element_type=F32)
        if at > 0:
            row_sum = running * decay + row_sum
            mixed = acc * jnp.concatenate([decay, decay], axis=1) + mixed
        old, running, acc = new, row_sum, mixed
        if at + size == KEYS:
            out.append((acc[:, 0:128] + acc[:, 128:256]) / jnp.sum(running, axis=1, keepdims=True))
            if s == 1:
                asend[0] = join_halves(out[0], True, out[1], True).astype(BF16).reshape(NY, ROWS, 128)
                go_home(0)
    asend[1] = out[2].astype(BF16).reshape(NY, ROWS, 128)
    go_home(1)

    for k in range(1, NY):
        plane = (y + k) % NY
        received(fhome.at[plane], f_s.at[k], f_r.at[plane])
    for b in range(2):
        blocks = []
        for h in range(HEADS):
            g, s = (h // UNITS, h % UNITS)
            blocks.append(fhome[2 * g + b, :, s * 128 : s * 128 + 128].astype(F32))
        magnitudes = []
        for kind in range(2):
            tiles = [join_halves(blocks[2 * m], kind == 1, blocks[2 * m + 1], kind == 1) for m in range(5)]
            top = jnp.abs(tiles[0])
            for tile in tiles[1:]:
                top = jnp.maximum(top, jnp.abs(tile))
            magnitude = jnp.max(top, axis=1, keepdims=True) + 1e-06
            magnitudes.append(magnitude)
            for m in range(5):
                at = kind * 640 + m * 128
                fvals_ref[b, :, at : at + 128] = (tiles[m] / magnitude).astype(BF16)
        both = jnp.concatenate(magnitudes, axis=1).astype(BF16)
        turned = lax.dot_general(both, eye, (((0,), (0,)), ((), ())), preferred_element_type=F32)
        fscales_ref[b] = turned.astype(BF16)

    for part in range(2):
        for k in range(1, NY):
            plane = (y + k) % NY
            received(ahome.at[part, plane], a_s.at[part, k], a_r.at[part, plane])
    for b in range(2):
        pairs = [ahome[0, 2 * g + b].astype(F32) for g in range(4)]
        lasts = [ahome[1, 2 * g + b].astype(F32) for g in range(4)]
        att_ref[b, :, 0:128] = pairs[0].astype(BF16)
        att_ref[b, :, 128:256] = join_halves(lasts[0], True, pairs[1], False).astype(BF16)
        att_ref[b, :, 256:384] = join_halves(pairs[1], True, lasts[1], True).astype(BF16)
        att_ref[b, :, 384:512] = pairs[2].astype(BF16)
        att_ref[b, :, 512:640] = join_halves(lasts[2], True, pairs[3], False).astype(BF16)

    for finish in pending:
        finish()


def write_out(a, b, c, d, a_out, b_out, c_out, d_out, a_mid, b_mid, c_mid, d_mid, sems):
    mids = (a_mid, b_mid, c_mid, d_mid)
    steps = []
    for k, src in enumerate((a, b, c, d)):
        steps.append(pltpu.make_async_copy(src, mids[k], sems.at[k]))
        steps[k].start()
    out = []
    for k, dst in enumerate((a_out, b_out, c_out, d_out)):
        steps[k].wait()
        out.append(pltpu.make_async_copy(mids[k], dst, sems.at[4 + k]))
        out[k].start()
    for copy in out:
        copy.wait()


def local(hidden_in, gn_gain, gn_bias, stale_local, w_qkv, stale_values, stale_scales):
    dma = pltpu.SemaphoreType.DMA
    vmem = pltpu.VMEM
    scratch = [
        vmem((2, ROWS, D), BF16),
        vmem((D,), F32),
        vmem((D,), F32),
        vmem((4, GROUPS), F32),
        vmem((20, 1920), BF16),
        vmem((2, ROWS, D), BF16),
        vmem((2, 2, ROWS), BF16),
        dma((7,)),
        vmem((NY, CHUNK, 128), BF16),
        vmem((NZ, 2, NY, CHUNK, 128), BF16),
        vmem((UNITS, KEYS, 256), BF16),
        vmem((NY, ROWS, D), BF16),
        vmem((QROWS, D), BF16),
        vmem((8, 128), F32),
        vmem((NY, 8, 128), F32),
        vmem((2, 8, 128), F32),
        vmem((NZ, 8, 128), F32),
        vmem((32, 1920), F32),
        vmem((4, 32, WCOLS), BF16),
        vmem((128, WCOLS), BF16),
        vmem((80, WCOLS), BF16),
        vmem((D, WCOLS), BF16),
        vmem((UNITS, QROWS, 256), BF16),
        vmem((QROWS, 2 * QROWS), F32),
        vmem((NY, ROWS, 384), BF16),
        vmem((NY, ROWS, 384), BF16),
        vmem((2, NY, ROWS, 128), BF16),
        vmem((2, NY, ROWS, 128), BF16),
        dma((NY,)),
        dma((NY,)),
        dma((NZ, 4)),
        dma((NZ, 4)),
        dma((NZ, 4)),
        dma((NZ, 4)),
        dma((NY + 1,)),
        dma((NY,)),
        dma((NY,)),
        dma((NY,)),
        dma(()),
        dma(()),
        dma((NZ,)),
        dma((NZ,)),
        dma((4,)),
        dma((4,)),
        dma((2,)),
        dma((1,)),
        dma((NZ,)),
        dma((NZ,)),
        dma((NZ, NX)),
        dma((NZ, NX)),
        dma((NZ,)),
        dma((NZ,)),
        dma((NY,)),
        dma((NY,)),
        dma((2, NY)),
        dma((2, NY)),
    ]
    whole = pl.BlockSpec(memory_space=pltpu.VMEM)
    anywhere = pl.BlockSpec(memory_space=pl.ANY)
    out_shape = (
        jax.ShapeDtypeStruct((2, ROWS, 640), BF16),
        jax.ShapeDtypeStruct((2, ROWS, D), BF16),
        jax.ShapeDtypeStruct((2, 2, ROWS), BF16),
        jax.ShapeDtypeStruct((4, GROUPS), F32),
    )
    results = pl.pallas_call(
        kernel,
        out_shape=out_shape,
        in_specs=[anywhere] * 7,
        out_specs=(whole,) * 4,
        scratch_shapes=scratch,
        compiler_params=pltpu.CompilerParams(
            collective_id=0, has_side_effects=True, vmem_limit_bytes=56 * 2**20
        ),
        name="attend_planes",
    )(
        hidden_in,
        gn_gain,
        gn_bias,
        stale_local.reshape(4, GROUPS),
        w_qkv,
        stale_values,
        jnp.transpose(stale_scales, (0, 2, 1)),
    )
    attended, fresh_values, fresh_scales, totals = pl.pallas_call(
        write_out,
        out_shape=out_shape,
        in_specs=[anywhere] * 4,
        out_specs=(anywhere,) * 4,
        scratch_shapes=[vmem(o.shape, o.dtype) for o in out_shape] + [dma((8,))],
        compiler_params=pltpu.CompilerParams(vmem_limit_bytes=62 * 2**20),
        name="write_out",
    )(*results)
    return attended, fresh_values, jnp.transpose(fresh_scales, (0, 2, 1)), totals.reshape(2, 2, GROUPS)


def solution(mesh):
    in_specs = (
        P("img", "patch", None),
        P(),
        P(),
        P("img", "patch", None, None),
        P("patch", None),
        P("img", "patch", None),
        P("img", "patch", None),
    )
    out_specs = (
        P("img", "patch", None),
        P("img", "patch", None),
        P("img", "patch", None),
        P("img", None, None),
    )
    return jax.shard_map(local, mesh=mesh, in_specs=in_specs, out_specs=out_specs, check_vma=False)
```

```python
import jax
import jax.numpy as jnp
from jax import lax
from jax.experimental import pallas as pl
from jax.experimental.pallas import tpu as pltpu
from jax.sharding import PartitionSpec as P

HEADS = 10
HEAD_DIM = 64
GROUPS = 32
D = 1280
CPG = 40
ROWS = 48
NY = 8
NZ = 4
NX = 4
QROWS = NY * ROWS
UNITS = 3
CHUNK = UNITS * ROWS + 16
WCOLS = 640
CELLS = 122880.0
KEYS = 9 * QROWS
BIG_NEG = -1e30
OFF = (0, 1, -1, 2, -2, 3, -3, 4)
KV_GROUPS = ((0, 1), (1, 2), (3, 2), (5, 3))
MESH = pl.DeviceIdType.MESH
F32 = jnp.float32
BF16 = jnp.bfloat16


def head_of(group, unit):
    return min(UNITS * group + unit, HEADS - 1)


def lane_low(shape):
    return lax.broadcasted_iota(jnp.int32, shape, 1) < HEAD_DIM


def join_halves(low, low_high, high, high_high):
    left = pltpu.roll(low, HEAD_DIM, 1) if low_high else low
    right = high if high_high else pltpu.roll(high, HEAD_DIM, 1)
    return jnp.where(lane_low(left.shape), left, right)


def kernel(
    hid_ref,
    gain_ref,
    bias_ref,
    stale_ref,
    w_ref,
    codes_ref,
    scales_ref,
    att_ref,
    fvals_ref,
    fscales_ref,
    totals_ref,
    hid,
    gain,
    bias,
    stale,
    w_own,
    codes,
    scales,
    in_sem,
    kvs,
    kv,
    kv2,
    xbuf,
    xn,
    st,
    stbuf,
    stsib,
    stz,
    w32,
    wpack,
    w0,
    w80,
    wbuf,
    qbuf,
    mask,
    fsend,
    fhome,
    asend,
    ahome,
    kvy_s,
    kvy_r,
    kvz_s,
    kvz_r,
    kvsib_s,
    kvsib_r,
    x_s,
    x_r,
    sty_s,
    sty_r,
    stsib_s,
    stsib_r,
    stz_s,
    stz_r,
    p0_s,
    p0_r,
    wy_s,
    wy_r,
    wz_s,
    wz_r,
    wx_s,
    wx_r,
    ws_s,
    ws_r,
    f_s,
    f_r,
    a_s,
    a_r,
):
    img = lax.axis_index("img")
    patch = lax.axis_index("patch")
    x = img % NX
    img_base = img - x
    z = patch // (2 * NY)
    y = (patch // 2) % NY
    c = patch % 2

    def dev(y_at=None, z_at=None, c_at=None, x_at=None):
        yy = y if y_at is None else y_at
        zz = z if z_at is None else z_at
        cc = c if c_at is None else c_at
        xx = x if x_at is None else x_at
        return {"img": img_base + xx, "patch": (zz * NY + yy) * 2 + cc}

    sib = dev(c_at=1 - c)
    y_peers = [dev(y_at=(y + k) % NY) for k in range(1, NY)]
    z_peers = [dev(z_at=(z + k) % NZ) for k in range(1, NZ)]
    x_peers = [dev(x_at=(x + k) % NX) for k in range(1, NX)]
    ring = (img // NX) * NZ + z

    def on_ring(step):
        at = (ring + step) % (2 * NZ)
        return {"img": (at // NZ) * NX + x, "patch": ((at % NZ) * NY + y) * 2 + c}

    ring_peers = [on_ring(step) for step in (1, -1, 2, -2)]
    y_twin = y + 1 - 2 * (y % 2)
    diag = dev(y_at=y_twin, c_at=1 - c)
    everyone = y_peers + z_peers + x_peers + ring_peers + [sib, diag]

    barrier = pltpu.get_barrier_semaphore()
    for peer in everyone:
        pl.semaphore_signal(barrier, inc=1, device_id=peer, device_id_type=MESH)

    img_b = y % 2
    active = (y // 2) == x
    four = (y % 2) * 2 + c
    w_core = c == (y // 2) % 2

    pending = []

    def send(src, dst, s_sem, r_sem, peer, when=None):
        copy = pltpu.make_async_remote_copy(
            src_ref=src, dst_ref=dst, send_sem=s_sem, recv_sem=r_sem, device_id=peer, device_id_type=MESH
        )

        def start():
            copy.start()

        def finish():
            copy.wait_send()

        if when is None:
            start()
            pending.append(finish)
        else:
            pl.when(when)(start)
            pending.append(lambda: pl.when(when)(finish))

    def received(dst, s_sem, r_sem):
        pltpu.make_async_remote_copy(
            src_ref=dst, dst_ref=dst, send_sem=s_sem, recv_sem=r_sem, device_id=sib, device_id_type=MESH
        ).wait_recv()

    copies = []
    sources = (codes_ref, w_ref, scales_ref, hid_ref, stale_ref, gain_ref, bias_ref)
    for k, (src, dst) in enumerate(zip(sources, (codes, w_own, scales, hid, stale, gain, bias))):
        copy = pltpu.make_async_copy(src, dst, in_sem.at[k])
        copy.start()
        copies.append(copy)
    copies[1].wait()

    @pl.when(active)
    def _():
        w32[...] = jnp.zeros_like(w32)
        w32[0:20, :] = w_own[...].astype(F32)

        def piece(block, head):
            unit = block * HEADS + head
            return w32[:, (unit // 2) * 128 : (unit // 2) * 128 + 128], unit % 2 == 1

        for g in range(4):
            h = [head_of(g, s) for s in range(UNITS)]
            plan = [((1, h[s]), (2, h[s])) for s in range(UNITS)]
            plan += [((0, h[0]), (0, h[1])), ((0, h[2]), (0, h[2]))]
            for t, (first, second) in enumerate(plan):
                a, a_high = piece(*first)
                b, b_high = piece(*second)
                wpack[g, :, t * 128 : t * 128 + 128] = join_halves(a, a_high, b, b_high).astype(BF16)

    copies[0].wait()
    copies[2].wait()
    eye_row = lax.broadcasted_iota(jnp.int32, (ROWS, ROWS), 0)
    eye_col = lax.broadcasted_iota(jnp.int32, (ROWS, ROWS), 1)
    eye = jnp.where(eye_row == eye_col, 1.0, 0.0).astype(BF16)
    for b in range(2):
        lane16 = lax.broadcasted_iota(jnp.int32, (16, 128), 1)
        sc = lax.dot_general(eye, scales[b], (((1,), (1,)), ((), ())), preferred_element_type=F32)
        tile = jnp.zeros((16, 128), F32)
        for t in range(3):
            for f in range(2):
                col = sc[t * 16 : t * 16 + 16, f : f + 1]
                tile = jnp.where(lane16 == 2 * t + f, col, tile)
        tile = tile.astype(BF16)
        packed = {}
        for h in range(HEADS):
            k_tile = codes[b, :, (h // 2) * 128 : (h // 2) * 128 + 128].astype(F32)
            v_tile = codes[b, :, 640 + (h // 2) * 128 : 640 + (h // 2) * 128 + 128].astype(F32)
            odd = h % 2 == 1
            packed[h] = join_halves(k_tile, odd, v_tile, odd).astype(BF16)
        for g in range(4):
            for s in range(UNITS):
                kvs[2 * g + b, s * ROWS : (s + 1) * ROWS, :] = packed[head_of(g, s)]
            kvs[2 * g + b, UNITS * ROWS : CHUNK, :] = tile

    copies[3].wait()
    copies[4].wait()
    sub = lax.broadcasted_iota(jnp.int32, (GROUPS, D), 0) * CPG
    lane = lax.broadcasted_iota(jnp.int32, (GROUPS, D), 1)
    spread = jnp.where((lane >= sub) & (lane < sub + CPG), 1.0, 0.0).astype(F32)
    col_sums = []
    for b in range(2):
        feats = hid[b].astype(F32)
        col_sums.append(jnp.sum(feats, axis=0, keepdims=True))
        col_sums.append(jnp.sum(feats * feats, axis=0, keepdims=True))
    col_sums = jnp.concatenate(col_sums, axis=0)
    fresh = lax.dot_general(
        col_sums, spread, (((1,), (1,)), ((), ())), precision=lax.Precision.HIGHEST, preferred_element_type=F32
    )
    st[...] = jnp.zeros_like(st)
    st[0:4, 0:GROUPS] = stale[...]
    st[4:8, 0:GROUPS] = fresh
    stbuf[y] = st[...]

    kv[z, c, 0] = kvs[y]
    xbuf[0] = hid[img_b]

    pl.semaphore_wait(barrier, len(everyone))

    for j in range(4):
        peer = dev(y_at=y - y % 2 + j // 2, c_at=j % 2)
        send(wpack.at[j], w0.at[pl.ds(pl.multiple_of(four * 32, 32), 32)], p0_s.at[j], p0_r.at[four], peer, active & (four != j))

    def kv_to_plane(i):
        send(kvs.at[(y - OFF[i]) % NY], kv.at[z, c, i], kvy_s.at[i], kvy_r.at[i], dev(y_at=(y - OFF[i]) % NY))

    for i in range(1, 5):
        kv_to_plane(i)
    for k in range(1, NY):
        send(st, stbuf.at[y], sty_s.at[k], sty_r.at[y], dev(y_at=(y + k) % NY))
    def kv_part(zz, cc, grp):
        first, count = KV_GROUPS[grp]
        return kv.at[zz, cc, pl.ds(first, count)]

    def kv_own(grp):
        first, count = KV_GROUPS[grp]
        for i in range(first, first + count):
            if i > 0:
                received(kv.at[z, c, i], kvy_s.at[i], kvy_r.at[i])
        part = kv_part(z, c, grp)
        for k in range(1, NZ):
            to = (z + k) % NZ
            near = jnp.abs(to - z) < NZ - 1
            send(part, part, kvz_s.at[k, grp], kvz_r.at[z, grp], dev(z_at=to), near)
        send(part, part, kvsib_s.at[z, grp], kvsib_r.at[z, grp], sib)

    z_next = jnp.where(z == 3, 2, z + 1)
    z_other = jnp.where(z == 0, 2, jnp.where(z == 3, 1, z - 1))
    z_far = jnp.where(z < 2, 3, 0)

    def kv_arrive(grp):
        for zz in (z_next, z_other, z_far):
            part = kv_part(zz, c, grp)
            received(part, kvz_s.at[1, grp], kvz_r.at[zz, grp])
            if zz is z_far:
                middle = (z == 1) | (z == 2)
                send(part, part, kvz_s.at[0, grp], kvz_r.at[zz, grp], dev(z_at=3 - z_far), middle)
            send(part, part, kvsib_s.at[zz, grp], kvsib_r.at[zz, grp], sib)

    own_zc = z * 2 + c
    low16 = lane_low((16, 128))

    def widen(zz, cc, grp):
        place = ((zz * 2 + cc - own_zc) % 8 + 1) * QROWS
        first, count = KV_GROUPS[grp]

        def body(slot, carry):
            scale_tile = kv[zz, cc, slot, UNITS * ROWS : CHUNK, :].astype(F32)
            for t in range(3):
                factor = jnp.where(low16, scale_tile[:, 2 * t : 2 * t + 1], scale_tile[:, 2 * t + 1 : 2 * t + 2])
                at = pl.ds(pl.multiple_of(place + slot * ROWS + t * 16, 16), 16)
                for s in range(UNITS):
                    code = kv[zz, cc, slot, s * ROWS + t * 16 : s * ROWS + t * 16 + 16, :].astype(F32)
                    wide = code * factor
                    high = wide.astype(BF16)
                    kv2[s, at, 0:128] = high
                    kv2[s, at, 128:256] = (wide - high.astype(F32)).astype(BF16)
            return carry

        lax.fori_loop(first, first + count, body, 0)

    def widen_far(grp):
        for zz in (z_next, z_other, z_far):
            widen(zz, c, grp)

    def from_sibling(zz, grp):
        received(kv_part(zz, 1 - c, grp), kvsib_s.at[zz, grp], kvsib_r.at[zz, grp])
        widen(zz, 1 - c, grp)

    def from_sibling_far(grp):
        for zz in (z_next, z_other, z_far):
            from_sibling(zz, grp)

    def x_send(src, i, peer, k, when=None):
        send(src, xbuf.at[i], x_s.at[k], x_r.at[i], peer, when)

    def x_wait(i):
        received(xbuf.at[i], x_s.at[i], x_r.at[i])

    def w_block(zz, xx):
        return wbuf.at[pl.ds(pl.multiple_of((zz * 4 + xx) * 80, 80), 80)]

    def w_along_x(zz):
        for k in range(1, NX):
            send(w_block(zz, x), w_block(zz, x), wx_s.at[zz, k], wx_r.at[zz, x], dev(x_at=(x + k) % NX), w_core)

    def w_four(zz):
        return wbuf.at[pl.ds(pl.multiple_of(zz * 320, 320), 320)]

    kv_own(0)

    for i in range(NY):
        lane_q = lax.broadcasted_iota(jnp.int32, (ROWS, QROWS), 1)
        same = (lane_q >= i * ROWS) & (lane_q < (i + 1) * ROWS)
        mask[i * ROWS : (i + 1) * ROWS, 0:QROWS] = jnp.where(same, 0.0, BIG_NEG)
        mask[i * ROWS : (i + 1) * ROWS, QROWS : 2 * QROWS] = jnp.where(same, BIG_NEG, 0.0)
    copies[5].wait()
    copies[6].wait()

    w_rows = pl.ds(pl.multiple_of((z * 4 + x) * 80, 80), 80)
    for j in range(4):

        @pl.when(active & (four != j))
        def _(j=j):
            received(w0.at[pl.ds(j * 32, 32)], p0_s.at[j], p0_r.at[j])

    @pl.when(active)
    def _():
        w0[pl.ds(pl.multiple_of(four * 32, 32), 32), :] = wpack[four]
        row = lax.broadcasted_iota(jnp.int32, (80, 128), 0)
        col = lax.broadcasted_iota(jnp.int32, (80, 128), 1)
        hit = jnp.zeros((80, 128), F32)
        for a in range(4):
            hit = jnp.where((row >= 20 * a) & (row < 20 * a + 20) & (col == row + 12 * a), 1.0, hit)
        w80[...] = jnp.dot(hit.astype(BF16), w0[...], preferred_element_type=F32).astype(BF16)

    for k in range(2):
        plane = 2 * four + k

        @pl.when(active & (plane == y))
        def _():
            wbuf[w_rows, :] = w80[...]

        send(w80, wbuf.at[w_rows], wy_s.at[k], wy_r.at[0], dev(y_at=plane), active & (plane != y))

    kv_own(1)

    for k in range(1, NY):
        yy = (y + k) % NY
        received(stbuf.at[yy], sty_s.at[k], sty_r.at[yy])
    y_sum = stbuf[0]
    for k in range(1, NY):
        y_sum = y_sum + stbuf[k]
    stsib[0] = y_sum
    send(stsib.at[0], stsib.at[1], stsib_s, stsib_r, sib)


    @pl.when(w_core & jnp.logical_not(active & (y // 2 == four)))
    def _():
        received(w_block(z, x), wy_s.at[0], wy_r.at[0])

    def w_rows_of(zz, first, count):
        return wbuf.at[pl.ds(pl.multiple_of((zz * 4 + x) * 80 + first, 16), count)]

    ring_parts = ((1, 0, 80), (-1, 0, 80), (2, 0, 48), (-2, 48, 32))
    for n, (step, first, count) in enumerate(ring_parts):
        mine = w_rows_of(z, first, count)
        send(mine, mine, wz_s.at[n], wz_r.at[n], on_ring(step), w_core)
    w_along_x(z)

    for i in range(5, NY):
        kv_to_plane(i)

    kv_own(2)

    for i in range(1, 5):
        dest = (y - OFF[i]) % NY
        x_send(hid.at[dest % 2], i, dev(y_at=dest), i)


    kv_arrive(0)

    for n, (step, first, count) in enumerate(ring_parts):
        zz = (z - step) % NZ

        @pl.when(w_core)
        def _(n=n, zz=zz, first=first, count=count):
            received(w_rows_of(zz, first, count), wz_s.at[n], wz_r.at[n])

        if n != 2:
            w_along_x(zz)

    kv_own(3)

    received(stsib.at[1], stsib_s, stsib_r)
    stz[z] = stsib[0] + stsib[1]
    for k in range(1, NZ):
        send(stz.at[z], stz.at[z], stz_s.at[k], stz_r.at[z], dev(z_at=(z + k) % NZ))


    for i in (1, 2):
        x_wait(i)
        x_send(xbuf.at[i], 4 + i, dev(y_at=(y - 2 * OFF[i]) % NY), 4 + i)

    kv_arrive(1)

    for grp in range(4):
        widen(z, c, grp)

    for i, core in ((3, 0), (4, 1)):
        x_wait(i)
        x_send(xbuf.at[i], 7, dev(y_at=(y - OFF[i]) % NY), 7 + core, c == core)

    kv_arrive(2)
    for grp in range(4):
        from_sibling(z, grp)

    for k in range(1, NZ):
        zz = (z + k) % NZ
        received(stz.at[zz], stz_s.at[k], stz_r.at[zz])
    total = stz[0]
    for k in range(1, NZ):
        total = total + stz[k]
    totals_ref[...] = total[4:8, 0:GROUPS]
    stat_rows = []
    for i in range(NY):
        own = stbuf[(y + OFF[i]) % NY]
        used = total[0:4, 0:GROUPS] - own[0:4, 0:GROUPS] + own[4:8, 0:GROUPS]
        used = jnp.where(img_b == 0, used[0:2], used[2:4])
        mean = used[0:1] / CELLS
        var = used[1:2] / CELLS - mean * mean
        stat_rows += [mean, lax.rsqrt(var + 1e-5)]
    stats = lax.dot_general(
        jnp.concatenate(stat_rows, axis=0),
        spread,
        (((1,), (0,)), ((), ())),
        precision=lax.Precision.HIGHEST,
        preferred_element_type=F32,
    )
    gain_row = gain[...].reshape(1, D)
    bias_row = bias[...].reshape(1, D)

    def normalise(i):
        feats = xbuf[i].astype(F32)
        normed = (feats - stats[2 * i : 2 * i + 1]) * stats[2 * i + 1 : 2 * i + 2]
        xn[i * ROWS : (i + 1) * ROWS, :] = (normed * gain_row + bias_row).astype(BF16)

    for i in range(5):
        normalise(i)

    for zz in range(NZ):
        for k in range(1, NX):
            xx = (x + k) % NX

            @pl.when(w_core)
            def _(zz=zz, xx=xx):
                received(w_block(zz, xx), wx_s.at[zz, 1], wx_r.at[zz, xx])

        send(w_four(zz), w_four(zz), ws_s.at[zz], ws_r.at[zz], sib, w_core)
    for grp in range(3):
        widen_far(grp)
        from_sibling_far(grp)
    kv_arrive(3)

    for i in range(5, NY):
        x_wait(i)
        normalise(i)

    for zz in range(NZ):

        @pl.when(jnp.logical_not(w_core))
        def _(zz=zz):
            received(w_four(zz), ws_s.at[zz], ws_r.at[zz])

    fsend[...] = jnp.dot(xn[...], wbuf[:, 0:384], preferred_element_type=F32).astype(BF16).reshape(NY, ROWS, 384)
    for i in range(1, NY):
        home = (y + OFF[i]) % NY
        send(fsend.at[i], fhome.at[y], f_s.at[i], f_r.at[y], dev(y_at=home))
    fhome[y] = fsend[0]
    q_all = jnp.dot(xn[...], wbuf[:, 384:640], preferred_element_type=F32).astype(BF16).astype(F32) * 0.125
    low = lane_low((QROWS, 128))
    for s in range(UNITS):
        part = q_all[:, 0:128] if s < 2 else q_all[:, 128:256]
        if s == 1:
            part = pltpu.roll(part, HEAD_DIM, 1)
        part = jnp.where(low, part, 0.0).astype(BF16)
        qbuf[s, :, 0:128] = part
        qbuf[s, :, 128:256] = part
        kv2[s, 0:QROWS, 0:128] = fsend[:, :, s * 128 : s * 128 + 128].reshape(QROWS, 128)
        kv2[s, 0:QROWS, 128:256] = jnp.zeros((QROWS, 128), BF16)

    widen_far(3)
    from_sibling_far(3)

    jobs = [(s, at, min(2 * QROWS, KEYS - at)) for s in range(UNITS) for at in range(0, KEYS, 2 * QROWS)]

    def scores_of(s, at, size):
        found = lax.dot_general(
            qbuf[s], kv2[s, at : at + size, :], (((1,), (1,)), ((), ())), preferred_element_type=F32
        )
        return found + mask[...] if at == 0 else found

    def go_home(k):
        for i in range(NY - 1, 0, -1):
            home = (y + OFF[i]) % NY
            send(asend.at[k, i], ahome.at[k, y], a_s.at[k, i], a_r.at[k, y], dev(y_at=home))
        ahome[k, y] = asend[k, 0]

    upcoming = scores_of(*jobs[0])
    out = []
    for n, (s, at, size) in enumerate(jobs):
        scores = upcoming
        if n + 1 < len(jobs):
            upcoming = scores_of(*jobs[n + 1])
        top = jnp.max(scores, axis=1, keepdims=True)
        if at == 0:
            new = jnp.broadcast_to(top, (QROWS, 128))
        else:
            new = jnp.maximum(old, top)
            decay = jnp.exp(old - new)
        lifted = jnp.exp(scores - jnp.concatenate([new] * (size // 128), axis=1))
        row_sum = lifted[:, 0:128]
        for k in range(1, size // 128):
            row_sum = row_sum + lifted[:, k * 128 : k * 128 + 128]
        mixed = jnp.dot(lifted.astype(BF16), kv2[s, at : at + size, :], preferred_element_type=F32)
        if at > 0:
            row_sum = running * decay + row_sum
            mixed = acc * jnp.concatenate([decay, decay], axis=1) + mixed
        old, running, acc = new, row_sum, mixed
        if at + size == KEYS:
            out.append((acc[:, 0:128] + acc[:, 128:256]) / jnp.sum(running, axis=1, keepdims=True))
            if s == 1:
                asend[0] = join_halves(out[0], True, out[1], True).astype(BF16).reshape(NY, ROWS, 128)
                go_home(0)
    asend[1] = out[2].astype(BF16).reshape(NY, ROWS, 128)
    drained = list(pending)
    go_home(1)
    for finish in drained:
        finish()

    for k in range(1, NY):
        plane = (y + k) % NY
        received(fhome.at[plane], f_s.at[k], f_r.at[plane])
    for b in range(2):
        blocks = []
        for h in range(HEADS):
            g, s = (h // UNITS, h % UNITS)
            blocks.append(fhome[2 * g + b, :, s * 128 : s * 128 + 128].astype(F32))
        magnitudes = []
        for kind in range(2):
            tiles = [join_halves(blocks[2 * m], kind == 1, blocks[2 * m + 1], kind == 1) for m in range(5)]
            top = jnp.abs(tiles[0])
            for tile in tiles[1:]:
                top = jnp.maximum(top, jnp.abs(tile))
            magnitude = jnp.max(top, axis=1, keepdims=True) + 1e-06
            magnitudes.append(magnitude)
            for m in range(5):
                at = kind * 640 + m * 128
                fvals_ref[b, :, at : at + 128] = (tiles[m] / magnitude).astype(BF16)
        both = jnp.concatenate(magnitudes, axis=1).astype(BF16)
        turned = lax.dot_general(both, eye, (((0,), (0,)), ((), ())), preferred_element_type=F32)
        fscales_ref[b] = turned.astype(BF16)

    for part in range(2):
        for k in range(1, NY):
            plane = (y + k) % NY
            received(ahome.at[part, plane], a_s.at[part, k], a_r.at[part, plane])
    for b in range(2):
        pairs = [ahome[0, 2 * g + b].astype(F32) for g in range(4)]
        lasts = [ahome[1, 2 * g + b].astype(F32) for g in range(4)]
        att_ref[b, :, 0:128] = pairs[0].astype(BF16)
        att_ref[b, :, 128:256] = join_halves(lasts[0], True, pairs[1], False).astype(BF16)
        att_ref[b, :, 256:384] = join_halves(pairs[1], True, lasts[1], True).astype(BF16)
        att_ref[b, :, 384:512] = pairs[2].astype(BF16)
        att_ref[b, :, 512:640] = join_halves(lasts[2], True, pairs[3], False).astype(BF16)

    for finish in pending[len(drained) :]:
        finish()


def write_out(a, b, c, d, a_out, b_out, c_out, d_out, a_mid, b_mid, c_mid, d_mid, sems):
    mids = (a_mid, b_mid, c_mid, d_mid)
    steps = []
    for k, src in enumerate((a, b, c, d)):
        steps.append(pltpu.make_async_copy(src, mids[k], sems.at[k]))
        steps[k].start()
    out = []
    for k, dst in enumerate((a_out, b_out, c_out, d_out)):
        steps[k].wait()
        out.append(pltpu.make_async_copy(mids[k], dst, sems.at[4 + k]))
        out[k].start()
    for copy in out:
        copy.wait()


def local(hidden_in, gn_gain, gn_bias, stale_local, w_qkv, stale_values, stale_scales):
    dma = pltpu.SemaphoreType.DMA
    vmem = pltpu.VMEM
    scratch = [
        vmem((2, ROWS, D), BF16),
        vmem((D,), F32),
        vmem((D,), F32),
        vmem((4, GROUPS), F32),
        vmem((20, 1920), BF16),
        vmem((2, ROWS, D), BF16),
        vmem((2, 2, ROWS), BF16),
        dma((7,)),
        vmem((NY, CHUNK, 128), BF16),
        vmem((NZ, 2, NY, CHUNK, 128), BF16),
        vmem((UNITS, KEYS, 256), BF16),
        vmem((NY, ROWS, D), BF16),
        vmem((QROWS, D), BF16),
        vmem((8, 128), F32),
        vmem((NY, 8, 128), F32),
        vmem((2, 8, 128), F32),
        vmem((NZ, 8, 128), F32),
        vmem((32, 1920), F32),
        vmem((4, 32, WCOLS), BF16),
        vmem((128, WCOLS), BF16),
        vmem((80, WCOLS), BF16),
        vmem((D, WCOLS), BF16),
        vmem((UNITS, QROWS, 256), BF16),
        vmem((QROWS, 2 * QROWS), F32),
        vmem((NY, ROWS, 384), BF16),
        vmem((NY, ROWS, 384), BF16),
        vmem((2, NY, ROWS, 128), BF16),
        vmem((2, NY, ROWS, 128), BF16),
        dma((NY,)),
        dma((NY,)),
        dma((NZ, 4)),
        dma((NZ, 4)),
        dma((NZ, 4)),
        dma((NZ, 4)),
        dma((NY + 1,)),
        dma((NY,)),
        dma((NY,)),
        dma((NY,)),
        dma(()),
        dma(()),
        dma((NZ,)),
        dma((NZ,)),
        dma((4,)),
        dma((4,)),
        dma((2,)),
        dma((1,)),
        dma((NZ,)),
        dma((NZ,)),
        dma((NZ, NX)),
        dma((NZ, NX)),
        dma((NZ,)),
        dma((NZ,)),
        dma((NY,)),
        dma((NY,)),
        dma((2, NY)),
        dma((2, NY)),
    ]
    whole = pl.BlockSpec(memory_space=pltpu.VMEM)
    anywhere = pl.BlockSpec(memory_space=pl.ANY)
    out_shape = (
        jax.ShapeDtypeStruct((2, ROWS, 640), BF16),
        jax.ShapeDtypeStruct((2, ROWS, D), BF16),
        jax.ShapeDtypeStruct((2, 2, ROWS), BF16),
        jax.ShapeDtypeStruct((4, GROUPS), F32),
    )
    results = pl.pallas_call(
        kernel,
        out_shape=out_shape,
        in_specs=[anywhere] * 7,
        out_specs=(whole,) * 4,
        scratch_shapes=scratch,
        compiler_params=pltpu.CompilerParams(
            collective_id=0, has_side_effects=True, vmem_limit_bytes=56 * 2**20
        ),
        name="attend_planes",
    )(
        hidden_in,
        gn_gain,
        gn_bias,
        stale_local.reshape(4, GROUPS),
        w_qkv,
        stale_values,
        jnp.transpose(stale_scales, (0, 2, 1)),
    )
    attended, fresh_values, fresh_scales, totals = pl.pallas_call(
        write_out,
        out_shape=out_shape,
        in_specs=[anywhere] * 4,
        out_specs=(anywhere,) * 4,
        scratch_shapes=[vmem(o.shape, o.dtype) for o in out_shape] + [dma((8,))],
        compiler_params=pltpu.CompilerParams(vmem_limit_bytes=62 * 2**20),
        name="write_out",
    )(*results)
    return attended, fresh_values, jnp.transpose(fresh_scales, (0, 2, 1)), totals.reshape(2, 2, GROUPS)


def solution(mesh):
    in_specs = (
        P("img", "patch", None),
        P(),
        P(),
        P("img", "patch", None, None),
        P("patch", None),
        P("img", "patch", None),
        P("img", "patch", None),
    )
    out_specs = (
        P("img", "patch", None),
        P("img", "patch", None),
        P("img", "patch", None),
        P("img", None, None),
    )
    return jax.shard_map(local, mesh=mesh, in_specs=in_specs, out_specs=out_specs, check_vma=False)
```
